256 devices in a mesh: dom: 16 (over y, x), feat: 16 (over z, core).
Axes of the slice: x: 4, y: 4, z: 8, core: 2. Of those that a mesh axis runs over, the one named last changes fastest.
Arguments:
- feature_table: float32 [1024, 131072], P('feat', 'dom'), may hold values from -6 to 6
- seed_ids: int32 [16384], P('dom'), may hold values from 0 to 8191
- neighbours: int32 [15, 16384], P(None, 'dom'), may hold values from 0 to 8191
- owners: int32 [1024, 1], P('dom'), may hold values from 0 to 15; in each aligned block of 64 rows (0 to 63, 64 to 127, ...) at most 8 rows name the same one
- blocks: int32 [1024], P('dom'), may hold values from 0 to 63
- counts: int32 [1024], P('dom'), may hold values from 1 to 128
- w_self: float32 [1024, 1024], P('feat'), may hold values from -0.1875 to 0.1875
- w_neigh: float32 [1024, 1024], P('feat'), may hold values from -0.5 to 0.5
- out_bias: float32 [1024], replicated, may hold values from -3 to 3
- cotangent: bfloat16 [16384, 1024], P(('dom', 'feat')), may hold values from -0.046875 to 0.046875
Outputs:
- hidden: bfloat16 [16384, 1024], P(('dom', 'feat'))
- grad_self: float32 [1024, 1024], P('feat')
- grad_neigh: float32 [1024, 1024], P('feat')
The draws below stay inside these ranges and needn't reach their ends.
Inputs may be any that keep to these rules, and one draw needn't show every extreme that they name: `owners`: among the 64 frontier entries of one partition no owner appears more than 8 times.
All inputs are finite; a program needn't handle non-finite values.
Results may differ from the reference program's by a relative error of at most 0.003.
Values may be sent and summed in bfloat16 or wider, within the bound.
No kernel may reach another device: no remote copies, remote signals or barrier semaphores. Data moves between devices by JAX's collectives and lax.ppermute only.
A program may use at most 128 MiB of HBM per device.

```python
import math
import jax
import jax.numpy as jnp
import numpy as np
from jax import lax

F = 1024
H = 1024
S_DEV = 1024
FAN = 15
BLOCK = 128
BLOCKS_DEV = 64
SLOTS = 8
FRONT = 64
SEEDS = 16384
NODES = 131072
N_DOM = 16


def set_ends(result, key, least, largest):
    longest = result.shape.index(max(result.shape))
    spots = []
    for shift in (0, 1):
        where = [jax.random.randint(jax.random.fold_in(key, axis), (), 0, length) for axis, length in enumerate(result.shape)]
        where[longest] = (where[longest] + shift) % result.shape[longest]
        spots.append(tuple(where))
    return result.at[spots[0]].set(least).at[spots[1]].set(largest)


def block_scale(key, dims, split, low, largest):
    def one(position, parts):
        heights = jax.random.uniform(jax.random.fold_in(jax.random.fold_in(key, 6), position), (parts,), jnp.float32, low / len(split), largest / len(split))
        return jnp.repeat(jnp.exp(heights), dims[position] // parts).reshape((-1,) + (1,) * (len(dims) - position - 1))

    loudness = one(*split[0])
    for cut in split[1:]:
        loudness = loudness * one(*cut)
    return loudness


def deal_out(own_key, own, number, rows, number_of, top, reach, skew):
    sequence = jax.random.permutation(own_key, number_of)
    crowded, common = portions_of(number_of, rows * top, reach, skew, True), portions_of(number_of, rows * top, reach, skew, False)
    places = jnp.arange(number_of)

    def named(tallies, offset_by):
        used = int((tallies > 0).sum())
        fixed = max(1, used // 4)
        moved = fixed + (places - fixed + offset_by * (used - fixed)) % max(1, number_of - fixed)
        return jnp.zeros((number_of,), jnp.int32).at[sequence[jnp.where(places < fixed, places, moved)]].set(jnp.asarray(tallies, jnp.int32))

    tallies = jnp.where(number % 4 == 0, named(crowded, number // 4), named(common, number - number // 4 - 1))
    mixed = jax.random.permutation(jax.random.fold_in(own, 3), number_of)
    donor, sink = mixed[0:number_of // 2 * 2:2], mixed[1:number_of // 2 * 2:2]
    slack = jnp.minimum(tallies[donor] - 1, reach - tallies[sink]) // 2
    slack = jnp.where((donor == sequence[0]) | (sink == sequence[0]) | (tallies[sink] == 0), 0, jnp.maximum(slack, 0))
    moved = jax.random.randint(jax.random.fold_in(own, 4), (number_of // 2,), 0, 1 << 20) % (slack + 1)
    tallies = tallies.at[donor].add(-moved).at[sink].add(moved)
    items = jnp.searchsorted(jnp.cumsum(tallies), jnp.arange(rows * top), side="right").astype(jnp.int32)
    table = items.reshape(top, rows).T
    table = table[jax.random.permutation(jax.random.fold_in(own, 1), rows)]
    offset_by = jax.random.randint(jax.random.fold_in(own, 2), (rows, 1), 0, top)
    return jnp.take_along_axis(table, (jnp.arange(top)[None, :] + offset_by) % top, axis=1)


def portions_of(count, total, limit, lean, full):
    loads = [(1 << 20) // math.isqrt(rank ** lean) + 1 for rank in range(1, count + 1)]
    largest = limit if full else min(limit, max(-(-total // count), total * loads[0] // sum(loads)))
    least = 1 if total - largest >= count - 1 else 0
    holding, spare = [largest] + [least] * (count - 1), total - largest - least * (count - 1)
    while spare > 0:
        candidates = [i for i in range(1, count) if holding[i] < largest] or [i for i in range(1, count) if holding[i] < limit]
        pool, left = sum([loads[i] for i in candidates]), spare
        for i in candidates:
            addition = min(limit - holding[i], max(1, left * loads[i] // pool), spare)
            holding[i] = holding[i] + addition
            spare = spare - addition
    return np.array(holding)


def bell_draw(rng, shape, width, most, split=(), kind=jnp.bfloat16):
    array = width * jax.random.normal(rng, shape, jnp.float32)
    if split:
        array = array * block_scale(rng, shape, split, -0.22, 0.18)
    return jnp.clip(array, -most, most).astype(kind)


def setup_inputs(seed: int = 0) -> dict:
    keys = jax.random.split(jax.random.key(seed), 11)
    feature_table = bell_draw(keys[0], (F, NODES), 1.0, 6.0, ((0, 16), (1, 16)), jnp.float32)
    seed_ids = set_ends(jax.random.randint(keys[1], (SEEDS,), 0, BLOCKS_DEV * BLOCK), jax.random.fold_in(keys[1], 1), 0, (BLOCKS_DEV * BLOCK) - 1).astype(jnp.int32)
    neighbours = set_ends(jax.random.randint(keys[2], (FAN, SEEDS), 0, FRONT * BLOCK), jax.random.fold_in(keys[2], 1), 0, (FRONT * BLOCK) - 1).astype(jnp.int32)
    owners_keys = jax.random.split(jax.random.fold_in(keys[3], 1), (N_DOM * FRONT) // FRONT)
    owners_turns = jax.random.permutation(jax.random.fold_in(keys[3], 3), (N_DOM * FRONT) // FRONT)
    owners = jax.vmap(lambda own, number: deal_out(jax.random.fold_in(keys[3], 2), own, number, FRONT, N_DOM, 1, SLOTS, 2))(owners_keys, owners_turns).reshape((N_DOM * FRONT, 1))
    blocks = set_ends(jax.random.randint(keys[4], (N_DOM * FRONT,), 0, BLOCKS_DEV), jax.random.fold_in(keys[4], 1), 0, BLOCKS_DEV - 1).astype(jnp.int32)
    counts = set_ends(jax.random.randint(keys[5], (N_DOM * FRONT,), 1, BLOCK + 1), jax.random.fold_in(keys[5], 1), 1, BLOCK).astype(jnp.int32)
    w_self = bell_draw(keys[6], (F, H), F ** -0.5, 0.1875, ((0, 16),), jnp.float32)
    w_neigh = bell_draw(keys[7], (F, H), (F // 8) ** -0.5, 0.5, ((0, 16),), jnp.float32)
    out_bias = bell_draw(keys[8], (H,), 0.5, 3.0, (), jnp.float32)
    cotangent = bell_draw(keys[9], (SEEDS, H), ((N_DOM * S_DEV) ** -0.5), 0.046875, ((0, 256),))
    return dict(feature_table=feature_table, seed_ids=seed_ids, neighbours=neighbours, owners=owners, blocks=blocks, counts=counts, w_self=w_self, w_neigh=w_neigh, out_bias=out_bias, cotangent=cotangent)


def silu_slope(preact):
    sigma = jax.nn.sigmoid(preact)
    return sigma * (1.0 + preact * (1.0 - sigma))


def contract(left, right):
    return lax.dot_general(left, right, (((0,), (0,)), ((), ())), precision=lax.Precision.HIGHEST, preferred_element_type=jnp.float32)


def reference(feature_table, seed_ids, neighbours, owners, blocks, counts, w_self, w_neigh, out_bias, cotangent):
    block_view = feature_table.reshape(F, N_DOM * BLOCKS_DEV, BLOCK)
    node_rows = BLOCKS_DEV * BLOCK
    inputs_all = (jnp.arange(N_DOM, dtype=jnp.int32), seed_ids.reshape(N_DOM, S_DEV),
                  neighbours.reshape(FAN, N_DOM, S_DEV).transpose(1, 0, 2), owners.reshape(N_DOM, FRONT),
                  blocks.reshape(N_DOM, FRONT), counts.reshape(N_DOM, FRONT), cotangent.reshape(N_DOM, S_DEV, H))

    def one_partition(grads, inputs_one):
        index, seeds, neighbour_ids, owner_ids, block_ids, row_counts, upstream = inputs_one
        frontier = block_view[:, owner_ids * BLOCKS_DEV + block_ids, :]
        row_valid = jnp.arange(BLOCK, dtype=jnp.int32)[None, :] < row_counts[:, None]
        frontier = jnp.where(row_valid[None], frontier, 0.0).reshape(F, FRONT * BLOCK)
        neighbour_sum = frontier[:, neighbour_ids[0]]
        for which in range(1, FAN):
            neighbour_sum = neighbour_sum + frontier[:, neighbour_ids[which]]
        neighbour_mean = neighbour_sum * (1.0 / FAN)
        self_rows = feature_table[:, index * node_rows + seeds]
        preact = contract(self_rows, w_self) + contract(neighbour_mean, w_neigh) + out_bias[None, :]
        hidden_part = jax.nn.silu(preact).astype(jnp.bfloat16)
        slope = (upstream.astype(jnp.float32) * silu_slope(preact)).astype(jnp.bfloat16)
        slope_wide = slope.astype(jnp.float32)
        grad_self_part = lax.dot_general(self_rows, slope_wide, (((1,), (0,)), ((), ())), precision=lax.Precision.HIGHEST, preferred_element_type=jnp.float32)
        grad_neigh_part = lax.dot_general(neighbour_mean, slope_wide, (((1,), (0,)), ((), ())), precision=lax.Precision.HIGHEST, preferred_element_type=jnp.float32)
        return (grads[0] + grad_self_part, grads[1] + grad_neigh_part), hidden_part

    start_grads = (jnp.zeros((F, H), jnp.float32), jnp.zeros((F, H), jnp.float32))
    grads, hidden_all = lax.scan(one_partition, start_grads, inputs_all)
    return hidden_all.reshape(SEEDS, H), grads[0], grads[1]
```

```python
import functools

import jax
import jax.numpy as jnp
from jax import lax
from jax.experimental import pallas as pl
from jax.experimental.pallas import tpu as pltpu
from jax.sharding import PartitionSpec as P

FAN = 15
BLOCK = 128
SLOTS = 8
HALF = BLOCK // 2
F32 = jnp.float32
BF16 = jnp.bfloat16
SMEM = pl.BlockSpec(memory_space=pltpu.SMEM)
VMEM = pl.BlockSpec(memory_space=pltpu.VMEM)


def lane_of(shape):
    return lax.broadcasted_iota(jnp.int32, shape, len(shape) - 1)


def split(value):
    high = value.astype(BF16)
    low = (value - high.astype(F32)).astype(BF16)
    return high, low


def dot(left, right):
    return jnp.dot(left, right, preferred_element_type=F32)


def prepare_kernel(core_ref, seed_ref, table_ref, packed_ref, self_ref, rows):
    core = core_ref[0]
    blocks = table_ref.shape[1] // BLOCK
    first = lane_of((HALF, BLOCK)) < HALF

    def turn(pair, carry):
        start = pl.multiple_of(pair * 2 * BLOCK, 2 * BLOCK)
        left = table_ref[:, pl.ds(start, BLOCK)]
        right = table_ref[:, pl.ds(start + BLOCK, BLOCK)]
        turned = jnp.concatenate([left, right], axis=0).T
        rows[pl.ds(start, BLOCK), :] = turned
        rows[pl.ds(start + BLOCK, BLOCK), :] = pltpu.roll(turned, HALF, 1)
        for which in range(2):
            near = pl.multiple_of(start + which * BLOCK + core * HALF, HALF)
            far = pl.multiple_of(start + (1 - which) * BLOCK + (1 - core) * HALF, HALF)
            both = jnp.where(first, rows[pl.ds(near, HALF), :], rows[pl.ds(far, HALF), :])
            packed_ref[2 * pair + which] = both.astype(BF16)
        return carry

    lax.fori_loop(0, blocks // 2, turn, 0, unroll=2)

    lane = lane_of((1, BLOCK)) < HALF

    def pick(group, carry):
        for step in range(32):
            lead = seed_ref[group * 64 + step + 32 * core]
            trail = seed_ref[group * 64 + step + 32 * (1 - core)]
            low = rows[pl.ds(lead, 1), :]
            high = rows[pl.ds(lax.bitwise_xor(trail, BLOCK), 1), :]
            self_ref[lax.rem(group, 2), lax.div(group, 2), pl.ds(step, 1), :] = jnp.where(lane, low, high)
        return carry

    lax.fori_loop(0, seed_ref.shape[0] // 64, pick, 0)


def pack_kernel(me_ref, request_ref, packed_ref, out_ref, wanted, wanted_smem, sem):
    me = me_ref[0]
    request = request_ref[...]
    parts = request.shape[0]
    lane = lane_of(request.shape)
    mine = jnp.logical_and(request == me, lane < HALF)
    below = lax.broadcasted_iota(jnp.int32, (BLOCK, BLOCK), 0) <= lane_of((BLOCK, BLOCK))
    rank = dot(mine.astype(BF16), below.astype(BF16))
    block = pltpu.roll(request, HALF, 1).astype(F32)
    result = jnp.zeros(request.shape, F32)
    for slot in range(SLOTS):
        hit = jnp.logical_and(mine, rank == slot + 1.0)
        chosen = jnp.sum(jnp.where(hit, block, 0.0), axis=1, keepdims=True)
        result = jnp.where(lane == slot, chosen, result)
    wanted[...] = result.astype(jnp.int32)
    copy = pltpu.make_async_copy(wanted, wanted_smem, sem)
    copy.start()
    copy.wait()

    def send(part, carry):
        for slot in range(SLOTS):
            out_ref[part, slot] = packed_ref[wanted_smem[part, slot]]
        return carry

    lax.fori_loop(0, parts, send, 0)


def gather_kernel(core_ref, owner_ref, count_ref, near_ref, own_ref, other_ref, out_ref, front, seen):
    core = core_ref[0]
    n_dom = own_ref.shape[0] // SLOTS
    for owner in range(n_dom):
        seen[owner] = 0
    lane = lane_of((HALF, BLOCK))
    row = lax.broadcasted_iota(jnp.int32, (HALF, BLOCK), 0)
    straight = (lane < HALF) == (core == 0)

    def place(entry, carry):
        owner = owner_ref[entry]
        rank = seen[owner]
        seen[owner] = rank + 1
        slot = owner * SLOTS + rank
        own = own_ref[slot].astype(F32)
        other = other_ref[slot].astype(F32)
        count = count_ref[entry]
        upper = jnp.where(straight, own, other)
        lower = pltpu.roll(jnp.where(straight, other, own), HALF, 1)
        start = pl.multiple_of(entry * BLOCK, BLOCK)
        front[pl.ds(start, HALF), :] = jnp.where(row < count, upper, 0.0)
        front[pl.ds(start + HALF, HALF), :] = jnp.where(row < count - HALF, lower, 0.0)
        return carry

    lax.fori_loop(0, owner_ref.shape[0], place, 0, unroll=4)

    def average(step, carry):
        group, part = lax.div(step, 4), lax.rem(step, 4)
        base = ((2 * group + core) * 64 + part * 16) * FAN
        for seed in range(16):
            terms = [front[pl.ds(near_ref[base + seed * FAN + k], 1), :] for k in range(FAN)]
            while len(terms) > 1:
                terms = [
                    terms[i] + terms[i + 1] if i + 1 < len(terms) else terms[i]
                    for i in range(0, len(terms), 2)
                ]
            out_ref[group, pl.ds(part * 16 + seed, 1), :] = terms[0] * (1.0 / FAN)
        return carry

    lax.fori_loop(0, 32, average, 0)


def join_kernel(core_ref, own_ref, other_ref, out_ref):
    straight = (lane_of((32, BLOCK)) < HALF) == (core_ref[0] == 0)
    for group in range(8):
        own, other = own_ref[group], other_ref[group]
        out_ref[group, :32] = jnp.where(straight, own, other)
        out_ref[group, 32:] = pltpu.roll(jnp.where(straight, other, own), HALF, 1)


def three(left, right_high, right_low):
    high, low = split(left)
    return dot(high, right_high) + (dot(high, right_low) + dot(low, right_high))


def self_kernel(self_ref, weight_ref, bias_ref, part_ref, high_ref, low_ref):
    part_ref[...] = jnp.broadcast_to(bias_ref[...], part_ref.shape)
    for step in range(4):
        left = jnp.concatenate([self_ref[2 * step], self_ref[2 * step + 1]], axis=1)
        own = jnp.concatenate([weight_ref[4 * step + i, :64] for i in range(4)], axis=0)
        part_ref[...] += three(left, *split(own))
        for i in range(4):
            high, low = split(weight_ref[4 * step + i, 64:])
            start = (4 * step + i) * 64
            high_ref[start : start + 64, :] = high
            low_ref[start : start + 64, :] = low


def forward_kernel(mean_ref, part_ref, high_ref, low_ref, cotangent_ref, hidden_ref, slope_ref):
    left = jnp.concatenate([mean_ref[i] for i in range(8)], axis=1)
    preact = part_ref[...] + three(left, high_ref[...], low_ref[...])
    sigma = 1.0 / (1.0 + jnp.exp(-preact))
    hidden_ref[...] = (preact * sigma).astype(BF16)
    slope = cotangent_ref[...].astype(F32) * (sigma * (1.0 + preact * (1.0 - sigma)))
    slope_ref[...] = slope.astype(BF16)


def gradient_kernel(ring_ref, self_ref, mean_ref, *rest):
    slopes, out_ref = rest[:8], rest[8]
    here = ring_ref[0]
    rows = [lax.rem(here - k + 8, 8) for k in range(8)]
    right = jnp.concatenate([ref[...] for ref in slopes], axis=0)
    for which, ref in enumerate((self_ref, mean_ref)):
        left = jnp.concatenate([ref[r] for r in rows], axis=0)
        total = 0.0
        for piece in split(left):
            total = total + lax.dot_general(
                piece, right, (((0,), (0,)), ((), ())), preferred_element_type=F32
            )
        for core in range(2):
            for chunk in range(8):
                start = core * 64 + chunk * 8
                out_ref[which * 8 + chunk, core] = total[start : start + 8]


def sum_kernel(core_ref, in_ref, keep_ref, send_ref):
    total = in_ref[0]
    for i in range(1, in_ref.shape[0]):
        total = total + in_ref[i]
    mine = core_ref[0] == 0
    keep_ref[...] = jnp.where(mine, total[0], total[1])
    send_ref[...] = jnp.where(mine, total[1], total[0])


def call(kernel, shapes, specs, scratch=(), limit=32, cost=None):
    return pl.pallas_call(
        kernel,
        out_shape=shapes,
        in_specs=specs,
        out_specs=jax.tree.map(lambda _: VMEM, shapes),
        scratch_shapes=list(scratch),
        cost_estimate=cost,
        compiler_params=pltpu.CompilerParams(vmem_limit_bytes=limit << 20),
    )


def cost(flops, size):
    return pl.CostEstimate(flops=flops, bytes_accessed=size, transcendentals=0)


def body(
    feature_table,
    seed_ids,
    neighbours,
    owners,
    blocks,
    counts,
    w_self,
    w_neigh,
    out_bias,
    cotangent,
):
    n_dom = lax.axis_size("dom")
    n_feat = lax.axis_size("feat")
    ring = n_feat // 2
    across = [(i, i ^ 1) for i in range(n_feat)]
    columns = [[2 * z + c for z in range(ring)] for c in range(2)]
    dom = lax.axis_index("dom").astype(jnp.int32).reshape(1)
    feat = lax.axis_index("feat").astype(jnp.int32).reshape(1)
    core, height = feat % 2, feat // 2
    hidden_width = w_self.shape[1]
    owner_ids = owners[:, 0]
    shape = jax.ShapeDtypeStruct

    weights = lax.all_gather(jnp.concatenate([w_self, w_neigh], axis=0), "feat", axis=0, tiled=False)

    request = jnp.concatenate([owner_ids, blocks])
    requests = lax.all_to_all(
        jnp.broadcast_to(request[None, None, :], (n_dom, 1, 2 * owner_ids.shape[0])),
        "dom", split_axis=0, concat_axis=0, tiled=True,
    ).reshape(n_dom, 2 * owner_ids.shape[0])

    packed, self_halves = call(
        prepare_kernel,
        (shape((64, HALF, BLOCK), BF16), shape((2, ring, 32, BLOCK), F32)),
        [SMEM, SMEM, VMEM],
        [pltpu.VMEM((feature_table.shape[1], BLOCK), F32)],
        cost=cost(0, 12 << 20),
    )(core, seed_ids, feature_table)

    outgoing = call(
        pack_kernel,
        shape((n_dom, SLOTS, HALF, BLOCK), BF16),
        [SMEM, VMEM, VMEM],
        [
            pltpu.VMEM((n_dom, BLOCK), jnp.int32),
            pltpu.SMEM((n_dom, BLOCK), jnp.int32),
            pltpu.SemaphoreType.DMA,
        ],
    )(dom, requests, packed)
    arrived = lax.all_to_all(
        outgoing.reshape(n_dom, SLOTS * HALF, BLOCK), "dom", split_axis=0, concat_axis=0, tiled=True
    )
    other = lax.ppermute(arrived, "feat", across)

    kept = lax.dynamic_index_in_dim(self_halves, core[0], 0, keepdims=False)
    given = lax.dynamic_index_in_dim(self_halves, 1 - core[0], 0, keepdims=False)
    self_rows = call(join_kernel, shape((ring, 64, BLOCK), F32), [SMEM, VMEM, VMEM])(
        core, kept, lax.ppermute(given, "feat", across)
    )
    self_seeds = lax.all_to_all(
        self_rows, "feat", split_axis=0, concat_axis=0, tiled=True, axis_index_groups=columns
    )
    part, high, low = call(
        self_kernel,
        (
            shape((64, hidden_width), F32),
            shape((64 * n_feat, hidden_width), BF16),
            shape((64 * n_feat, hidden_width), BF16),
        ),
        [VMEM, VMEM, VMEM],
        limit=40,
        cost=cost(3 << 27, 12 << 20),
    )(self_seeds, weights, out_bias[None, :])

    mean = call(
        gather_kernel,
        shape((ring, 64, BLOCK), F32),
        [SMEM, SMEM, SMEM, SMEM, VMEM, VMEM],
        [pltpu.VMEM((owner_ids.shape[0] * BLOCK, BLOCK), F32), pltpu.SMEM((n_dom,), jnp.int32)],
        cost=cost(0, 30 << 20),
    )(
        core,
        owner_ids,
        counts,
        jnp.transpose(neighbours).reshape(-1),
        arrived.reshape(n_dom * SLOTS, HALF, BLOCK),
        other.reshape(n_dom * SLOTS, HALF, BLOCK),
    )
    mean_seeds = lax.all_to_all(
        mean, "feat", split_axis=0, concat_axis=0, tiled=True, axis_index_groups=columns
    )

    hidden, slope = call(
        forward_kernel,
        (shape((64, hidden_width), BF16), shape((64, hidden_width), BF16)),
        [VMEM] * 5,
    )(mean_seeds, part, high, low, cotangent)

    slopes = [slope]
    for shift in range(1, ring):
        slopes.append(lax.ppermute(slope, "feat", [(i, (i + 2 * shift) % n_feat) for i in range(n_feat)]))

    partial = call(
        gradient_kernel, shape((n_dom, 2, 8, hidden_width), F32), [SMEM] + [VMEM] * 10
    )(height, self_rows, mean, *slopes)
    shares = lax.all_to_all(
        partial.reshape(n_dom, 16, hidden_width), "dom", split_axis=0, concat_axis=0, tiled=True
    )
    keep, send = call(
        sum_kernel,
        (shape((8, hidden_width), F32), shape((8, hidden_width), F32)),
        [SMEM, VMEM],
    )(core, shares.reshape(n_dom, 2, 8, hidden_width))
    total = keep + lax.ppermute(send, "feat", across)
    grads = lax.all_to_all(
        jnp.broadcast_to(total[None], (n_dom, 8, hidden_width)), "dom", split_axis=0, concat_axis=0, tiled=True
    ).reshape(n_dom * 8, hidden_width)
    return hidden, grads[: n_dom * 4], grads[n_dom * 4 :]


def solution(mesh):
    return jax.shard_map(
        body,
        mesh=mesh,
        in_specs=(
            P("feat", "dom"),
            P("dom"),
            P(None, "dom"),
            P("dom", None),
            P("dom"),
            P("dom"),
            P("feat", None),
            P("feat", None),
            P(),
            P(("dom", "feat"), None),
        ),
        out_specs=(P(("dom", "feat"), None), P("feat", None), P("feat", None)),
        check_vma=False,
    )
```

```python
import jax
import jax.numpy as jnp
from jax import lax
from jax.experimental import pallas as pl
from jax.experimental.pallas import tpu as pltpu
from jax.sharding import PartitionSpec as P

FAN = 15
BLOCK = 128
SLOTS = 8
HALF = BLOCK // 2
DISTANCES = (0, 1, -1, 2, -2, 3, -3, 4)
F32 = jnp.float32
BF16 = jnp.bfloat16
SMEM = pl.BlockSpec(memory_space=pltpu.SMEM)
VMEM = pl.BlockSpec(memory_space=pltpu.VMEM)
ANY = pl.BlockSpec(memory_space=pl.ANY)


def lane_of(shape):
    return lax.broadcasted_iota(jnp.int32, shape, len(shape) - 1)


def split(value):
    high = value.astype(BF16)
    low = (value - high.astype(F32)).astype(BF16)
    return high, low


def dot(left, right):
    return jnp.dot(left, right, preferred_element_type=F32)


def prepare_kernel(
    core_ref, seed_hbm, table_hbm, packed_ref, keep_ref, send_ref,
    rows, table, seed_ref, packed, sems, seed_sem, out_sems,
):
    core = core_ref[0]
    parts = sems.shape[0]
    width = table.shape[1] // parts
    pairs = width // (2 * BLOCK)
    first = lane_of((HALF, BLOCK)) < HALF

    def fetch(part):
        window = pl.ds(part * width, width)
        return pltpu.make_async_copy(table_hbm.at[:, window], table.at[:, window], sems.at[part])

    seeds = pltpu.make_async_copy(seed_hbm, seed_ref, seed_sem)
    seeds.start()
    for part in range(parts):
        fetch(part).start()

    def turn(pair, carry):
        start = pl.multiple_of(pair * 2 * BLOCK, 2 * BLOCK)
        left = table[:, pl.ds(start, BLOCK)]
        right = table[:, pl.ds(start + BLOCK, BLOCK)]
        turned = jnp.concatenate([left, right], axis=0).T
        rows[pl.ds(start, BLOCK), :] = turned
        rows[pl.ds(start + BLOCK, BLOCK), :] = pltpu.roll(turned, HALF, 1)
        for which in range(2):
            near = pl.multiple_of(start + which * BLOCK + core * HALF, HALF)
            far = pl.multiple_of(start + (1 - which) * BLOCK + (1 - core) * HALF, HALF)
            both_halves = jnp.where(first, rows[pl.ds(near, HALF), :], rows[pl.ds(far, HALF), :])
            packed[2 * pair + which] = both_halves.astype(BF16)
        return carry

    outs = []
    for part in range(parts):
        fetch(part).wait()
        lax.fori_loop(part * pairs, (part + 1) * pairs, turn, 0, unroll=2)
        window = pl.ds(2 * pairs * part, 2 * pairs)
        outs.append(pltpu.make_async_copy(packed.at[window], packed_ref.at[window], out_sems.at[part]))
        outs[-1].start()
    lane = lane_of((1, BLOCK)) < HALF
    seeds.wait()

    def pick(chip, carry):
        for mine, ref in ((True, keep_ref), (False, send_ref)):
            group = 2 * chip + (core if mine else 1 - core)
            for step in range(32):
                lead = seed_ref[group * 64 + step + 32 * core]
                trail = seed_ref[group * 64 + step + 32 * (1 - core)]
                low = rows[pl.ds(lead, 1), :]
                high = rows[pl.ds(lax.bitwise_xor(trail, BLOCK), 1), :]
                ref[chip, pl.ds(step, 1), :] = jnp.where(lane, low, high)
        return carry

    lax.fori_loop(0, keep_ref.shape[0], pick, 0)
    for copy in outs:
        copy.wait()


def pack_kernel(me_ref, request_ref, packed_hbm, out_hbm, wanted, wanted_smem, packed_ref, out_ref, sem, in_sem, out_sems):
    fetch = pltpu.make_async_copy(packed_hbm, packed_ref, in_sem)
    fetch.start()
    me = me_ref[0]
    request = request_ref[...]
    parts = request.shape[0]
    lane = lane_of(request.shape)
    mine = jnp.logical_and(request == me, lane < HALF)
    below = lax.broadcasted_iota(jnp.int32, (BLOCK, BLOCK), 0) <= lane_of((BLOCK, BLOCK))
    rank = dot(mine.astype(BF16), below.astype(BF16))
    block = pltpu.roll(request, HALF, 1).astype(F32)
    result = jnp.zeros(request.shape, F32)
    for slot in range(SLOTS):
        hit = jnp.logical_and(mine, rank == slot + 1.0)
        chosen = jnp.sum(jnp.where(hit, block, 0.0), axis=1, keepdims=True)
        result = jnp.where(lane == slot, chosen, result)
    wanted[...] = result.astype(jnp.int32)
    copy = pltpu.make_async_copy(wanted, wanted_smem, sem)
    copy.start()
    copy.wait()

    fetch.wait()
    copies = []
    for part in range(parts):
        for slot in range(SLOTS):
            out_ref[part, slot] = packed_ref[wanted_smem[part, slot]]
        copies.append(pltpu.make_async_copy(out_ref.at[part], out_hbm.at[part], out_sems.at[part]))
        copies[-1].start()
    for copy in copies:
        copy.wait()


def collect_kernel(owner_ref, arrived_ref, *rest):
    out_ref, seen = rest[-2:]
    for owner in range(arrived_ref.shape[0] // SLOTS):
        seen[owner] = 0

    def place(entry, carry):
        owner = owner_ref[entry]
        rank = seen[owner]
        seen[owner] = rank + 1
        out_ref[entry] = arrived_ref[owner * SLOTS + rank]
        return carry

    lax.fori_loop(0, out_ref.shape[0], place, 0, unroll=4)


def gather_kernel(core_ref, count_ref, near_ref, own_ref, other_ref, out_ref, front):
    core = core_ref[0]
    lane = lane_of((HALF, BLOCK))
    row = lax.broadcasted_iota(jnp.int32, (HALF, BLOCK), 0)
    straight = (lane < HALF) == (core == 0)

    def place(entry, carry):
        own = own_ref[entry].astype(F32)
        other = other_ref[entry].astype(F32)
        count = count_ref[entry]
        upper = jnp.where(straight, own, other)
        lower = pltpu.roll(jnp.where(straight, other, own), HALF, 1)
        start = pl.multiple_of(entry * BLOCK, BLOCK)
        front[pl.ds(start, HALF), :] = jnp.where(row < count, upper, 0.0)
        front[pl.ds(start + HALF, HALF), :] = jnp.where(row < count - HALF, lower, 0.0)
        return carry

    lax.fori_loop(0, own_ref.shape[0], place, 0, unroll=4)

    def average(step, carry):
        group, part = lax.div(step, 4), lax.rem(step, 4)
        base = ((2 * group + core) * 64 + part * 16) * FAN
        for seed in range(16):
            terms = [front[pl.ds(near_ref[base + seed * FAN + k], 1), :] for k in range(FAN)]
            while len(terms) > 1:
                terms = [
                    terms[i] + terms[i + 1] if i + 1 < len(terms) else terms[i]
                    for i in range(0, len(terms), 2)
                ]
            out_ref[group, pl.ds(part * 16 + seed, 1), :] = terms[0] * (1.0 / FAN)
        return carry

    lax.fori_loop(0, 32, average, 0)


def join_kernel(place_ref, own_ref, other_ref, *rest):
    out_ref, sends = rest[0], rest[1:]
    straight = (lane_of((32, BLOCK)) < HALF) == (place_ref[0] == 0)
    ring = own_ref.shape[0]
    for shift in range(ring):
        group = lax.rem(place_ref[1] + shift, ring)
        own, other = own_ref[group], other_ref[group]
        upper = jnp.where(straight, own, other)
        lower = pltpu.roll(jnp.where(straight, other, own), HALF, 1)
        out_ref[group, :32] = upper
        out_ref[group, 32:] = lower
        target = sends[shift]
        target[:32] = upper
        target[32:] = lower


def weight_kernel(self_hbm, neigh_hbm, out_ref, both, sems):
    copies = [
        pltpu.make_async_copy(ref, both.at[which], sems.at[which])
        for which, ref in enumerate((self_hbm, neigh_hbm))
    ]
    for copy in copies:
        copy.start()
    copies[0].wait()
    high, low = split(both[0])
    out_ref[0] = high
    out_ref[1] = low
    copies[1].wait()
    out_ref[2] = both[1].astype(BF16)


def three(left, right_high, right_low):
    high, low = split(left)
    return dot(high, right_high) + (dot(high, right_low) + dot(low, right_high))


def self_kernel(place_ref, bias_ref, weight_hbm, *rest):
    pieces = rest[:8]
    part_ref, neigh_ref, held, rows, sems, row_sems = rest[8:]
    row_copies = [
        pltpu.make_async_copy(piece, rows.at[index], row_sems.at[index]) for index, piece in enumerate(pieces)
    ]
    for copy in row_copies:
        copy.start()
    chips = [lax.rem(place_ref[1] + 8 - distance, 8) for distance in DISTANCES]
    copies = []
    for index, chip in enumerate(chips):
        pair = weight_hbm.at[pl.ds(2 * chip, 2), pl.ds(0, 2)]
        copies.append(pltpu.make_async_copy(pair, held.at[index], sems.at[index]))
        copies[-1].start()
    neigh_copies = []
    for core in range(16):
        target = neigh_ref.at[core]
        neigh_copies.append(pltpu.make_async_copy(weight_hbm.at[core, 2], target, sems.at[8 + core]))
        neigh_copies[-1].start()
    part_ref[...] = jnp.broadcast_to(bias_ref[...], part_ref.shape)
    for step in range(4):
        pair = (2 * step, 2 * step + 1)
        for index in pair:
            copies[index].wait()
            row_copies[index].wait()
        left = jnp.concatenate([rows[index] for index in pair], axis=1)
        high, low = [
            jnp.concatenate([held[index, core, which] for index in pair for core in range(2)], axis=0)
            for which in range(2)
        ]
        part_ref[...] += three(left, high, low)
    for copy in neigh_copies:
        copy.wait()


def forward_kernel(mean_ref, part_ref, weight_ref, cotangent_ref, hidden_ref, slope_ref):
    preact = part_ref[...]
    left = jnp.concatenate([mean_ref[chip] for chip in range(8)], axis=1)
    right = weight_ref[...]
    for piece in split(left):
        preact += dot(piece, right)
    sigma = 1.0 / (1.0 + jnp.exp(-preact))
    hidden_ref[...] = (preact * sigma).astype(BF16)
    slope = cotangent_ref[...].astype(F32) * (sigma * (1.0 + preact * (1.0 - sigma)))
    slope_ref[...] = slope.astype(BF16)


def gradient_kernel(place_ref, self_ref, mean_ref, near_ref, *rest):
    slopes, (keep_ref, send_ref) = rest[:-2], rest[-2:]
    here = place_ref[1]
    rows = [lax.rem(here - k + 8, 8) for k in DISTANCES]
    right = jnp.concatenate([near_ref[...]] + [ref[...] for ref in slopes], axis=0)
    first = place_ref[0] == 0
    for which, ref in enumerate((self_ref, mean_ref)):
        left = jnp.concatenate([ref[r] for r in rows], axis=0)
        total = 0.0
        for piece in split(left):
            total = total + lax.dot_general(
                piece, right, (((0,), (0,)), ((), ())), preferred_element_type=F32
            )
        for chunk in range(8):
            start = chunk * 8
            one, two = total[start : start + 8], total[64 + start : 64 + start + 8]
            keep_ref[which * 8 + chunk] = jnp.where(first, one, two)
            send_ref[which * 8 + chunk] = jnp.where(first, two, one)


def add_kernel(left_ref, right_ref, out_ref):
    out_ref[...] = left_ref[...] + right_ref[...]


def sum_kernel(in_ref, out_ref):
    total = in_ref[0]
    for i in range(1, in_ref.shape[0]):
        total = total + in_ref[i]
    for i in range(out_ref.shape[0]):
        out_ref[i] = total


def call(kernel, shapes, specs, scratch=(), limit=8, cost=None, outs=None, aliases={}):
    return pl.pallas_call(
        kernel,
        out_shape=shapes,
        in_specs=specs,
        out_specs=outs or jax.tree.map(lambda _: VMEM, shapes),
        input_output_aliases=aliases,
        scratch_shapes=list(scratch),
        cost_estimate=cost,
        compiler_params=pltpu.CompilerParams(vmem_limit_bytes=limit << 20),
    )


def cost(flops, size):
    return pl.CostEstimate(flops=flops, bytes_accessed=size, transcendentals=0)


def body(
    feature_table,
    seed_ids,
    neighbours,
    owners,
    blocks,
    counts,
    w_self,
    w_neigh,
    out_bias,
    cotangent,
):
    n_dom = lax.axis_size("dom")
    n_feat = lax.axis_size("feat")
    ring = n_feat // 2
    across = [(i, i ^ 1) for i in range(n_feat)]
    columns = [[2 * z + c for z in range(ring)] for c in range(2)]
    dom = lax.axis_index("dom").astype(jnp.int32).reshape(1)
    feat = lax.axis_index("feat").astype(jnp.int32).reshape(1)
    core = feat % 2
    place = jnp.concatenate([core, feat // 2])
    hidden_width = w_self.shape[1]

    def climb(value, chips):
        pairs = [(i, (i + 2 * chips) % n_feat) for i in range(n_feat)]
        return lax.ppermute(value, "feat", pairs)

    owner_ids = owners[:, 0]
    shape = jax.ShapeDtypeStruct

    request = jnp.concatenate([owner_ids, blocks])
    requests = lax.all_to_all(
        jnp.broadcast_to(request[None, None, :], (n_dom, 1, 2 * owner_ids.shape[0])),
        "dom", split_axis=0, concat_axis=0, tiled=True,
    ).reshape(n_dom, 2 * owner_ids.shape[0])
    near = jnp.transpose(neighbours).reshape(-1)
    weights = lax.all_gather(
        call(
            weight_kernel, shape((3, 64, hidden_width), BF16), [ANY, ANY],
            [pltpu.VMEM((2, 64, hidden_width), F32), pltpu.SemaphoreType.DMA((2,))], limit=60,
        )(w_self, w_neigh),
        "feat", axis=0, tiled=False,
    )

    packed, kept, given = call(
        prepare_kernel,
        (
            shape((feature_table.shape[1] // BLOCK, HALF, BLOCK), BF16),
            shape((ring, 32, BLOCK), F32),
            shape((ring, 32, BLOCK), F32),
        ),
        [SMEM, ANY, ANY],
        [
            pltpu.VMEM((feature_table.shape[1], BLOCK), F32),
            pltpu.VMEM(feature_table.shape, F32),
            pltpu.SMEM(seed_ids.shape, jnp.int32),
            pltpu.VMEM((feature_table.shape[1] // BLOCK, HALF, BLOCK), BF16),
            pltpu.SemaphoreType.DMA((4,)),
            pltpu.SemaphoreType.DMA,
            pltpu.SemaphoreType.DMA((4,)),
        ],
        limit=60, cost=cost(0, 10 << 20), outs=(ANY, VMEM, VMEM),
    )(core, seed_ids, feature_table)

    outgoing = call(
        pack_kernel,
        shape((n_dom, SLOTS, HALF, BLOCK), BF16),
        [SMEM, VMEM, ANY],
        [
            pltpu.VMEM((n_dom, BLOCK), jnp.int32),
            pltpu.SMEM((n_dom, BLOCK), jnp.int32),
            pltpu.VMEM(packed.shape, BF16),
            pltpu.VMEM((n_dom, SLOTS, HALF, BLOCK), BF16),
            pltpu.SemaphoreType.DMA,
            pltpu.SemaphoreType.DMA,
            pltpu.SemaphoreType.DMA((n_dom,)),
        ],
        limit=60, outs=ANY,
    )(dom, requests, packed)
    arrived = lax.all_to_all(
        outgoing.reshape(n_dom, SLOTS * HALF, BLOCK), "dom", split_axis=0, concat_axis=0, tiled=True
    )
    self_rows, *sends = call(
        join_kernel,
        (shape((ring, 64, BLOCK), F32),) + (shape((64, BLOCK), F32),) * ring,
        [SMEM, VMEM, VMEM],
        limit=60, cost=cost(0, 1 << 20),
    )(place, kept, lax.ppermute(given, "feat", across))
    moved = [climb(sends[k % ring], k) for k in DISTANCES[1:]]
    pieces = [sends[0]] + moved

    entries = call(
        collect_kernel, shape((owner_ids.shape[0], HALF, BLOCK), BF16),
        [SMEM, VMEM] + [ANY] * 8, [pltpu.SMEM((n_dom,), jnp.int32)], limit=2, cost=cost(0, 2 << 20),
    )(owner_ids, arrived.reshape(n_dom * SLOTS, HALF, BLOCK), *moved, near)
    mean = call(
        gather_kernel,
        shape((ring, 64, BLOCK), F32),
        [SMEM, SMEM, SMEM, VMEM, VMEM],
        [pltpu.VMEM((owner_ids.shape[0] * BLOCK, BLOCK), F32)],
        cost=cost(0, 30 << 20),
    )(core, counts, near, entries, lax.ppermute(entries, "feat", across))

    part, neigh_weight = call(
        self_kernel,
        (shape((64, hidden_width), F32), shape((n_feat, 64, hidden_width), BF16)),
        [SMEM, VMEM] + [ANY] * 9,
        [
            pltpu.VMEM((ring, 2, 2, 64, hidden_width), BF16),
            pltpu.VMEM((ring, 64, BLOCK), F32),
            pltpu.SemaphoreType.DMA((24,)),
            pltpu.SemaphoreType.DMA((ring,)),
        ],
        limit=56, cost=cost(3 << 27, 9 << 20),
    )(place, out_bias[None, :], weights, *pieces)
    mean_seeds = lax.all_to_all(
        mean, "feat", split_axis=0, concat_axis=0, tiled=True, axis_index_groups=columns
    )

    hidden, slope = call(
        forward_kernel,
        (shape((64, hidden_width), BF16), shape((64, hidden_width), BF16)),
        [VMEM] * 4, limit=8, cost=cost(2 << 27, 4 << 20),
    )(mean_seeds, part, neigh_weight.reshape(-1, hidden_width), cotangent)

    up, down = climb(slope, 1), climb(slope, -1)
    up_two, down_two = climb(slope, 2), climb(slope, -2)
    up_three, down_three = climb(up_two, 1), climb(down_two, -1)
    up_four, down_four = climb(up_two[:32], 2), climb(down_two[32:], -2)
    slopes = [up, down, up_two, down_two, up_three, down_three, up_four, down_four]

    keep, send = call(
        gradient_kernel, (shape((n_dom, 8, hidden_width), F32),) * 2, [SMEM] + [VMEM] * 11, limit=16
    )(place, self_rows, mean, slope, *slopes)
    partial = call(add_kernel, shape(keep.shape, F32), [VMEM, VMEM], limit=4)(
        keep, lax.ppermute(send, "feat", across)
    )
    shares = lax.all_to_all(partial, "dom", split_axis=0, concat_axis=0, tiled=True)
    total = call(sum_kernel, shape(shares.shape, F32), [VMEM], limit=4)(shares)
    grads = lax.all_to_all(
        total, "dom", split_axis=0, concat_axis=0, tiled=True
    ).reshape(n_dom * 8, hidden_width)
    return hidden, grads[: n_dom * 4], grads[n_dom * 4 :]


def solution(mesh):
    return jax.shard_map(
        body,
        mesh=mesh,
        in_specs=(
            P("feat", "dom"),
            P("dom"),
            P(None, "dom"),
            P("dom", None),
            P("dom"),
            P("dom"),
            P("feat", None),
            P("feat", None),
            P(),
            P(("dom", "feat"), None),
        ),
        out_specs=(P(("dom", "feat"), None), P("feat", None), P("feat", None)),
        check_vma=False,
    )
```

```python
import jax
import jax.numpy as jnp
from jax import lax
from jax.experimental import pallas as pl
from jax.experimental.pallas import tpu as pltpu
from jax.sharding import PartitionSpec as P

FAN = 15
BLOCK = 128
SLOTS = 8
HALF = BLOCK // 2
DISTANCES = (0, 1, -1, 2, -2, 3, -3, 4)
F32 = jnp.float32
BF16 = jnp.bfloat16
SMEM = pl.BlockSpec(memory_space=pltpu.SMEM)
VMEM = pl.BlockSpec(memory_space=pltpu.VMEM)
ANY = pl.BlockSpec(memory_space=pl.ANY)


def lane_of(shape):
    return lax.broadcasted_iota(jnp.int32, shape, len(shape) - 1)


def split(value):
    high = value.astype(BF16)
    low = (value - high.astype(F32)).astype(BF16)
    return high, low


def dot(left, right):
    return jnp.dot(left, right, preferred_element_type=F32)


def prepare_kernel(
    core_ref, seed_hbm, table_hbm, packed_ref, keep_ref, send_ref,
    rows, table, seed_ref, packed, sems, seed_sem, out_sems,
):
    core = core_ref[0]
    parts = sems.shape[0]
    width = table.shape[1] // parts
    pairs = width // (2 * BLOCK)
    first = lane_of((HALF, BLOCK)) < HALF

    def fetch(part):
        window = pl.ds(part * width, width)
        return pltpu.make_async_copy(table_hbm.at[:, window], table.at[:, window], sems.at[part])

    seeds = pltpu.make_async_copy(seed_hbm, seed_ref, seed_sem)
    seeds.start()
    for part in range(parts):
        fetch(part).start()

    def turn(pair, carry):
        start = pl.multiple_of(pair * 2 * BLOCK, 2 * BLOCK)
        left = table[:, pl.ds(start, BLOCK)]
        right = table[:, pl.ds(start + BLOCK, BLOCK)]
        turned = jnp.concatenate([left, right], axis=0).T
        rows[pl.ds(start, BLOCK), :] = turned
        rows[pl.ds(start + BLOCK, BLOCK), :] = pltpu.roll(turned, HALF, 1)
        for which in range(2):
            near = pl.multiple_of(start + which * BLOCK + core * HALF, HALF)
            far = pl.multiple_of(start + (1 - which) * BLOCK + (1 - core) * HALF, HALF)
            both_halves = jnp.where(first, rows[pl.ds(near, HALF), :], rows[pl.ds(far, HALF), :])
            packed[2 * pair + which] = both_halves.astype(BF16)
        return carry

    outs = []
    for part in range(parts):
        fetch(part).wait()
        lax.fori_loop(part * pairs, (part + 1) * pairs, turn, 0, unroll=2)
        window = pl.ds(2 * pairs * part, 2 * pairs)
        outs.append(pltpu.make_async_copy(packed.at[window], packed_ref.at[window], out_sems.at[part]))
        outs[-1].start()
    seeds.wait()

    def pick(chip, carry):
        for mine, ref in ((True, keep_ref), (False, send_ref)):
            base = (2 * chip + (core if mine else 1 - core)) * 64
            for step in range(64):
                ref[chip, pl.ds(step, 1), :] = rows[pl.ds(seed_ref[base + step], 1), :]
        return carry

    lax.fori_loop(0, keep_ref.shape[0], pick, 0)
    for copy in outs:
        copy.wait()


def pack_kernel(
    me_ref, request_ref, packed_hbm, self_hbm, neigh_hbm, out_hbm, weight_ref,
    wanted, wanted_smem, packed_ref, both, out_ref, sem, in_sem, out_sems, weight_sems,
):
    fetch = pltpu.make_async_copy(packed_hbm, packed_ref, in_sem)
    fetch.start()
    weights = [
        pltpu.make_async_copy(ref, both.at[which], weight_sems.at[which])
        for which, ref in enumerate((self_hbm, neigh_hbm))
    ]
    for copy in weights:
        copy.start()
    me = me_ref[0]
    request = request_ref[...]
    parts = request.shape[0]
    lane = lane_of(request.shape)
    mine = jnp.logical_and(request == me, lane < HALF)
    below = lax.broadcasted_iota(jnp.int32, (BLOCK, BLOCK), 0) <= lane_of((BLOCK, BLOCK))
    rank = dot(mine.astype(BF16), below.astype(BF16))
    block = pltpu.roll(request, HALF, 1).astype(F32)
    result = jnp.zeros(request.shape, F32)
    for slot in range(SLOTS):
        hit = jnp.logical_and(mine, rank == slot + 1.0)
        chosen = jnp.sum(jnp.where(hit, block, 0.0), axis=1, keepdims=True)
        result = jnp.where(lane == slot, chosen, result)
    wanted[...] = result.astype(jnp.int32)
    copy = pltpu.make_async_copy(wanted, wanted_smem, sem)
    copy.start()
    for held in weights:
        held.wait()
    high, low = split(both[0])
    weight_ref[0] = high
    weight_ref[1] = low
    weight_ref[2] = both[1].astype(BF16)
    copy.wait()
    fetch.wait()
    copies = []
    for part in range(parts):
        for slot in range(SLOTS):
            out_ref[part, slot] = packed_ref[wanted_smem[part, slot]]
        copies.append(pltpu.make_async_copy(out_ref.at[part], out_hbm.at[part], out_sems.at[part]))
        copies[-1].start()
    for copy in copies:
        copy.wait()


def collect_kernel(owner_ref, arrived_ref, *rest):
    out_ref, seen = rest[-2:]
    for owner in range(arrived_ref.shape[0] // SLOTS):
        seen[owner] = 0

    def place(entry, carry):
        owner = owner_ref[entry]
        rank = seen[owner]
        seen[owner] = rank + 1
        out_ref[entry] = arrived_ref[owner * SLOTS + rank]
        return carry

    lax.fori_loop(0, out_ref.shape[0], place, 0, unroll=4)


def gather_kernel(core_ref, count_ref, near_ref, own_ref, other_ref, out_ref, front):
    core = core_ref[0]
    lane = lane_of((HALF, BLOCK))
    row = lax.broadcasted_iota(jnp.int32, (HALF, BLOCK), 0)
    straight = (lane < HALF) == (core == 0)

    def place(entry, carry):
        own = own_ref[entry].astype(F32)
        other = other_ref[entry].astype(F32)
        count = count_ref[entry]
        upper = jnp.where(straight, own, other)
        lower = pltpu.roll(jnp.where(straight, other, own), HALF, 1)
        start = pl.multiple_of(entry * BLOCK, BLOCK)
        front[pl.ds(start, HALF), :] = jnp.where(row < count, upper, 0.0)
        front[pl.ds(start + HALF, HALF), :] = jnp.where(row < count - HALF, lower, 0.0)
        return carry

    lax.fori_loop(0, own_ref.shape[0], place, 0, unroll=4)

    def average(step, carry):
        group, part = lax.div(step, 4), lax.rem(step, 4)
        base = ((2 * group + core) * 64 + part * 16) * FAN
        for seed in range(16):
            terms = [front[pl.ds(near_ref[base + seed * FAN + k], 1), :] for k in range(FAN)]
            while len(terms) > 1:
                terms = [
                    terms[i] + terms[i + 1] if i + 1 < len(terms) else terms[i]
                    for i in range(0, len(terms), 2)
                ]
            out_ref[group, pl.ds(part * 16 + seed, 1), :] = terms[0] * (1.0 / FAN)
        return carry

    lax.fori_loop(0, 32, average, 0)


def join_kernel(place_ref, own_ref, other_ref, *rest):
    out_ref, sends = rest[0], rest[1:]
    lane = lane_of((64, BLOCK)) < HALF
    first = place_ref[0] == 0
    ring = own_ref.shape[0]
    for shift in range(ring):
        group = lax.rem(place_ref[1] + shift, ring)
        own, other = own_ref[group], other_ref[group]
        left, right = jnp.where(first, own, other), jnp.where(first, other, own)
        joined = jnp.where(lane, left, pltpu.roll(right, HALF, 1))
        out_ref[group] = joined
        sends[shift][...] = joined


def open_kernel(owner_ref, block_ref, request_ref):
    request = jnp.concatenate([owner_ref[...], block_ref[...]], axis=1)
    for part in range(request_ref.shape[0]):
        request_ref[part] = request


def three(left, right_high, right_low):
    high, low = split(left)
    return dot(high, right_high) + (dot(high, right_low) + dot(low, right_high))


def self_kernel(place_ref, bias_ref, weight_hbm, *rest):
    pieces = rest[:8]
    part_ref, neigh_ref, held, rows, sems, row_sems = rest[8:]
    chips = [lax.rem(place_ref[1] + 8 - distance, 8) for distance in DISTANCES]
    copies, row_copies = [], []
    for index, (piece, chip) in enumerate(zip(pieces, chips)):
        row_copies.append(pltpu.make_async_copy(piece, rows.at[index], row_sems.at[index]))
        row_copies[-1].start()
        pair = weight_hbm.at[pl.ds(2 * chip, 2), pl.ds(0, 2)]
        copies.append(pltpu.make_async_copy(pair, held.at[index], sems.at[index]))
        copies[-1].start()
    neigh_copies = []
    for step in range(4):
        window = pl.ds(4 * step, 4)
        neigh_copies.append(
            pltpu.make_async_copy(weight_hbm.at[window, 2], neigh_ref.at[window], sems.at[8 + step])
        )
        neigh_copies[-1].start()
    total = jnp.broadcast_to(bias_ref[...], part_ref.shape)
    for step in range(4):
        pair = (2 * step, 2 * step + 1)
        for index in pair:
            copies[index].wait()
            row_copies[index].wait()
        left = jnp.concatenate([rows[index] for index in pair], axis=1)
        high, low = [
            jnp.concatenate([held[index, core, which] for index in pair for core in range(2)], axis=0)
            for which in range(2)
        ]
        total = total + three(left, high, low)
    part_ref[...] = total
    for copy in neigh_copies:
        copy.wait()


def forward_kernel(mean_ref, part_ref, weight_ref, cotangent_ref, hidden_ref, slope_ref):
    preact = part_ref[...]
    for step in range(4):
        left = jnp.concatenate([mean_ref[2 * step], mean_ref[2 * step + 1]], axis=1)
        right = weight_ref[4 * step : 4 * step + 4].reshape(256, weight_ref.shape[2])
        for piece in split(left):
            preact = preact + dot(piece, right)
    sigma = 1.0 / (1.0 + jnp.exp(-preact))
    hidden_ref[...] = (preact * sigma).astype(BF16)
    slope = cotangent_ref[...].astype(F32) * (sigma * (1.0 + preact * (1.0 - sigma)))
    slope_ref[...] = slope.astype(BF16)


def turn_kernel(place_ref, self_ref, mean_ref, high_ref, low_ref):
    rows = [lax.rem(place_ref[1] + 8 - k, 8) for k in DISTANCES]
    for which, ref in enumerate((self_ref, mean_ref)):
        turned = jnp.concatenate([ref[r] for r in rows], axis=0).T
        window = slice(which * BLOCK, (which + 1) * BLOCK)
        high_ref[window], low_ref[window] = split(turned)


def gradient_kernel(place_ref, high_ref, low_ref, near_ref, *rest):
    slopes, (keep_ref, send_ref) = rest[:-2], rest[-2:]
    right = jnp.concatenate([near_ref[...]] + [ref[...] for ref in slopes], axis=0)
    first = place_ref[0] == 0
    for which in range(2):
        window = slice(which * BLOCK, (which + 1) * BLOCK)
        total = dot(high_ref[window], right) + dot(low_ref[window], right)
        for chunk in range(8):
            start = chunk * 8
            one, two = total[start : start + 8], total[64 + start : 64 + start + 8]
            keep_ref[which * 8 + chunk] = jnp.where(first, one, two)
            send_ref[which * 8 + chunk] = jnp.where(first, two, one)


def add_kernel(left_ref, right_ref, out_ref):
    out_ref[...] = left_ref[...] + right_ref[...]


def sum_kernel(in_ref, out_ref):
    total = in_ref[0]
    for i in range(1, in_ref.shape[0]):
        total = total + in_ref[i]
    for i in range(out_ref.shape[0]):
        out_ref[i] = total


def call(kernel, shapes, specs, scratch=(), limit=8, cost=None, outs=None, aliases={}):
    return pl.pallas_call(
        kernel,
        out_shape=shapes,
        in_specs=specs,
        out_specs=outs or jax.tree.map(lambda _: VMEM, shapes),
        input_output_aliases=aliases,
        scratch_shapes=list(scratch),
        cost_estimate=cost,
        compiler_params=pltpu.CompilerParams(vmem_limit_bytes=int(limit * (1 << 20))),
    )


def cost(flops, size):
    return pl.CostEstimate(flops=flops, bytes_accessed=size, transcendentals=0)


def body(
    feature_table,
    seed_ids,
    neighbours,
    owners,
    blocks,
    counts,
    w_self,
    w_neigh,
    out_bias,
    cotangent,
):
    n_dom = lax.axis_size("dom")
    n_feat = lax.axis_size("feat")
    ring = n_feat // 2
    across = [(i, i ^ 1) for i in range(n_feat)]
    columns = [[2 * z + c for z in range(ring)] for c in range(2)]
    dom = lax.axis_index("dom").astype(jnp.int32).reshape(1)
    feat = lax.axis_index("feat").astype(jnp.int32).reshape(1)
    core = feat % 2
    place = jnp.concatenate([core, feat // 2])
    hidden_width = w_self.shape[1]

    def climb(value, chips):
        pairs = [(i, (i + 2 * chips) % n_feat) for i in range(n_feat)]
        return lax.ppermute(value, "feat", pairs)

    owner_ids = owners[:, 0]
    shape = jax.ShapeDtypeStruct

    entries_here = owner_ids.shape[0]
    request = call(
        open_kernel, shape((n_dom, 1, 2 * entries_here), jnp.int32), [VMEM, VMEM], limit=60
    )(owner_ids[None, :], blocks[None, :])
    requests = lax.all_to_all(request, "dom", split_axis=0, concat_axis=0, tiled=True).reshape(
        n_dom, 2 * entries_here
    )
    near = jnp.transpose(neighbours).reshape(-1)
    packed, kept, given = call(
        prepare_kernel,
        (
            shape((feature_table.shape[1] // BLOCK, HALF, BLOCK), BF16),
            shape((ring, 64, BLOCK), F32),
            shape((ring, 64, BLOCK), F32),
        ),
        [SMEM, ANY, ANY],
        [
            pltpu.VMEM((feature_table.shape[1], BLOCK), F32),
            pltpu.VMEM(feature_table.shape, F32),
            pltpu.SMEM(seed_ids.shape, jnp.int32),
            pltpu.VMEM((feature_table.shape[1] // BLOCK, HALF, BLOCK), BF16),
            pltpu.SemaphoreType.DMA((8,)),
            pltpu.SemaphoreType.DMA,
            pltpu.SemaphoreType.DMA((8,)),
        ],
        limit=60, cost=cost(0, 10 << 20), outs=(ANY, VMEM, VMEM),
    )(core, seed_ids, feature_table)

    outgoing, weight = call(
        pack_kernel,
        (shape((n_dom, SLOTS, HALF, BLOCK), BF16), shape((3, 64, hidden_width), BF16)),
        [SMEM, VMEM, ANY, ANY, ANY],
        [
            pltpu.VMEM((n_dom, BLOCK), jnp.int32),
            pltpu.SMEM((n_dom, BLOCK), jnp.int32),
            pltpu.VMEM(packed.shape, BF16),
            pltpu.VMEM((2, 64, hidden_width), F32),
            pltpu.VMEM((n_dom, SLOTS, HALF, BLOCK), BF16),
            pltpu.SemaphoreType.DMA,
            pltpu.SemaphoreType.DMA,
            pltpu.SemaphoreType.DMA((n_dom,)),
            pltpu.SemaphoreType.DMA((2,)),
        ],
        limit=59, outs=(ANY, VMEM),
    )(dom, requests, packed, w_self, w_neigh)
    weights = lax.all_gather(weight, "feat", axis=0, tiled=False)
    arrived = lax.all_to_all(
        outgoing.reshape(n_dom, SLOTS * HALF, BLOCK), "dom", split_axis=0, concat_axis=0, tiled=True
    )
    self_rows, *sends = call(
        join_kernel,
        (shape((ring, 64, BLOCK), F32),) + (shape((64, BLOCK), F32),) * ring,
        [SMEM, VMEM, VMEM],
        limit=60, cost=cost(0, 1 << 20),
    )(place, kept, lax.ppermute(given, "feat", across))
    moved = [climb(sends[k % ring], k) for k in DISTANCES[1:]]
    pieces = [sends[0]] + moved

    entries = call(
        collect_kernel, shape((owner_ids.shape[0], HALF, BLOCK), BF16),
        [SMEM, VMEM] + [ANY] * 8, [pltpu.SMEM((n_dom,), jnp.int32)], limit=2, cost=cost(0, 2 << 20),
    )(owner_ids, arrived.reshape(n_dom * SLOTS, HALF, BLOCK), *moved, near)
    mean = call(
        gather_kernel,
        shape((ring, 64, BLOCK), F32),
        [SMEM, SMEM, SMEM, VMEM, VMEM],
        [pltpu.VMEM((owner_ids.shape[0] * BLOCK, BLOCK), F32)],
        cost=cost(0, 30 << 20),
    )(core, counts, near, entries, lax.ppermute(entries, "feat", across))

    part, neigh_weight = call(
        self_kernel,
        (shape((64, hidden_width), F32), shape((n_feat, 64, hidden_width), BF16)),
        [SMEM, VMEM] + [ANY] * 9,
        [
            pltpu.VMEM((ring, 2, 2, 64, hidden_width), BF16),
            pltpu.VMEM((ring, 64, BLOCK), F32),
            pltpu.SemaphoreType.DMA((12,)),
            pltpu.SemaphoreType.DMA((ring,)),
        ],
        limit=24, cost=cost(3 << 27, 9 << 20),
    )(place, out_bias[None, :], weights, *pieces)
    mean_seeds = lax.all_to_all(
        mean, "feat", split_axis=0, concat_axis=0, tiled=True, axis_index_groups=columns
    )

    hidden, slope = call(
        forward_kernel,
        (shape((64, hidden_width), BF16), shape((64, hidden_width), BF16)),
        [VMEM] * 4, limit=8, cost=cost(2 << 27, 4 << 20),
    )(mean_seeds, part, neigh_weight, cotangent)

    up, down = climb(slope, 1), climb(slope, -1)
    up_two, down_two = climb(slope, 2), climb(slope, -2)
    up_three, down_three = climb(up_two, 1), climb(down_two, -1)
    up_four, down_four = climb(up_two[:32], 2), climb(down_two[32:], -2)
    slopes = [up, down, up_two, down_two, up_three, down_three, up_four, down_four]

    turned = call(
        turn_kernel, (shape((2 * BLOCK, ring * 64), BF16),) * 2, [SMEM, VMEM, VMEM], limit=8
    )(place, self_rows, mean)
    keep, send = call(
        gradient_kernel, (shape((n_dom, 8, hidden_width), F32),) * 2, [SMEM] + [VMEM] * 11, limit=16
    )(place, *turned, slope, *slopes)
    partial = call(add_kernel, shape(keep.shape, F32), [VMEM, VMEM], limit=4)(
        keep, lax.ppermute(send, "feat", across)
    )
    shares = lax.all_to_all(partial, "dom", split_axis=0, concat_axis=0, tiled=True)
    total = call(sum_kernel, shape(shares.shape, F32), [VMEM], limit=4)(shares)
    grads = lax.all_to_all(
        total, "dom", split_axis=0, concat_axis=0, tiled=True
    ).reshape(n_dom * 8, hidden_width)
    return hidden, grads[: n_dom * 4], grads[n_dom * 4 :]


def solution(mesh):
    return jax.shard_map(
        body,
        mesh=mesh,
        in_specs=(
            P("feat", "dom"),
            P("dom"),
            P(None, "dom"),
            P("dom", None),
            P("dom"),
            P("dom"),
            P("feat", None),
            P("feat", None),
            P(),
            P(("dom", "feat"), None),
        ),
        out_specs=(P(("dom", "feat"), None), P("feat", None), P("feat", None)),
        check_vma=False,
    )
```

```python
import jax
import jax.numpy as jnp
from jax import lax
from jax.experimental import pallas as pl
from jax.experimental.pallas import tpu as pltpu
from jax.sharding import PartitionSpec as P

FAN = 15
BLOCK = 128
SLOTS = 8
HALF = BLOCK // 2
DISTANCES = (0, 1, -1, 2, -2, 3, -3, 4)
F32 = jnp.float32
BF16 = jnp.bfloat16
SMEM = pl.BlockSpec(memory_space=pltpu.SMEM)
VMEM = pl.BlockSpec(memory_space=pltpu.VMEM)
ANY = pl.BlockSpec(memory_space=pl.ANY)


def lane_of(shape):
    return lax.broadcasted_iota(jnp.int32, shape, len(shape) - 1)


def split(value):
    high = value.astype(BF16)
    low = (value - high.astype(F32)).astype(BF16)
    return high, low


def dot(left, right):
    return jnp.dot(left, right, preferred_element_type=F32)


def prepare_kernel(
    core_ref, seed_hbm, table_hbm, packed_ref, keep_ref, send_ref,
    rows, table, seed_ref, packed, sems, seed_sem, out_sems,
):
    core = core_ref[0]
    parts = sems.shape[0]
    width = table.shape[1] // parts
    pairs = width // (2 * BLOCK)
    first = lane_of((HALF, BLOCK)) < HALF

    def fetch(part):
        window = pl.ds(part * width, width)
        return pltpu.make_async_copy(table_hbm.at[:, window], table.at[:, window], sems.at[part])

    seeds = pltpu.make_async_copy(seed_hbm, seed_ref, seed_sem)
    seeds.start()
    for part in range(parts):
        fetch(part).start()

    def turn(pair, carry):
        start = pl.multiple_of(pair * 2 * BLOCK, 2 * BLOCK)
        left = table[:, pl.ds(start, BLOCK)]
        right = table[:, pl.ds(start + BLOCK, BLOCK)]
        turned = jnp.concatenate([left, right], axis=0).T
        rows[pl.ds(start, BLOCK), :] = turned
        rows[pl.ds(start + BLOCK, BLOCK), :] = pltpu.roll(turned, HALF, 1)
        for which in range(2):
            near = pl.multiple_of(start + which * BLOCK + core * HALF, HALF)
            far = pl.multiple_of(start + (1 - which) * BLOCK + (1 - core) * HALF, HALF)
            both_halves = jnp.where(first, rows[pl.ds(near, HALF), :], rows[pl.ds(far, HALF), :])
            packed[2 * pair + which] = both_halves.astype(BF16)
        return carry

    outs = []
    for part in range(parts):
        fetch(part).wait()
        lax.fori_loop(part * pairs, (part + 1) * pairs, turn, 0, unroll=pairs)
        window = pl.ds(2 * pairs * part, 2 * pairs)
        outs.append(pltpu.make_async_copy(packed.at[window], packed_ref.at[window], out_sems.at[part]))
        outs[-1].start()
    seeds.wait()

    def pick(chip, carry):
        for mine, ref in ((True, keep_ref), (False, send_ref)):
            base = (2 * chip + (core if mine else 1 - core)) * 64
            for step in range(64):
                ref[chip, pl.ds(step, 1), :] = rows[pl.ds(seed_ref[base + step], 1), :]
        return carry

    lax.fori_loop(0, keep_ref.shape[0], pick, 0)
    for copy in outs:
        copy.wait()


def pack_kernel(
    request_hbm, packed_hbm, self_hbm, neigh_hbm, out_hbm, weight_hbm,
    wanted, packed_ref, both, weight_ref, out_ref, sem, in_sem, out_sems, weight_sems,
):
    slots = pltpu.make_async_copy(request_hbm, wanted, sem)
    slots.start()
    fetch = pltpu.make_async_copy(packed_hbm, packed_ref, in_sem)
    fetch.start()
    weights = [
        pltpu.make_async_copy(ref, both.at[which], weight_sems.at[which])
        for which, ref in enumerate((self_hbm, neigh_hbm))
    ]
    for copy in weights:
        copy.start()
    for held in weights:
        held.wait()
    high, low = split(both[0])
    weight_ref[0] = high
    weight_ref[1] = low
    weight_ref[2] = both[1].astype(BF16)
    copies = [pltpu.make_async_copy(weight_ref, weight_hbm, weight_sems.at[2])]
    copies[0].start()
    slots.wait()
    fetch.wait()
    for part in range(out_ref.shape[0]):
        for slot in range(SLOTS):
            out_ref[part, slot] = packed_ref[wanted[part, 0, slot]]
        copies.append(pltpu.make_async_copy(out_ref.at[part], out_hbm.at[part], out_sems.at[part]))
        copies[-1].start()
    for copy in copies:
        copy.wait()


def collect_kernel(owner_ref, arrived_ref, *rest):
    out_ref, seen = rest[-2:]
    for owner in range(arrived_ref.shape[0] // SLOTS):
        seen[owner] = 0

    def place(entry, carry):
        owner = owner_ref[entry]
        rank = seen[owner]
        seen[owner] = rank + 1
        out_ref[entry] = arrived_ref[owner * SLOTS + rank]
        return carry

    lax.fori_loop(0, out_ref.shape[0], place, 0, unroll=8)


def gather_kernel(core_ref, count_ref, near_ref, own_ref, other_ref, out_ref, front):
    core = core_ref[0]
    lane = lane_of((HALF, BLOCK))
    row = lax.broadcasted_iota(jnp.int32, (HALF, BLOCK), 0)
    straight = (lane < HALF) == (core == 0)

    def place(entry, carry):
        own = own_ref[entry].astype(F32)
        other = other_ref[entry].astype(F32)
        count = count_ref[entry]
        upper = jnp.where(straight, own, other)
        lower = pltpu.roll(jnp.where(straight, other, own), HALF, 1)
        start = pl.multiple_of(entry * BLOCK, BLOCK)
        front[pl.ds(start, HALF), :] = jnp.where(row < count, upper, 0.0)
        front[pl.ds(start + HALF, HALF), :] = jnp.where(row < count - HALF, lower, 0.0)
        return carry

    lax.fori_loop(0, own_ref.shape[0], place, 0, unroll=8)

    def average(step, carry):
        group, part = lax.div(step, 2), lax.rem(step, 2)
        base = ((2 * group + core) * 64 + part * 32) * FAN
        for seed in range(32):
            terms = [front[pl.ds(near_ref[base + seed * FAN + k], 1), :] for k in range(FAN)]
            while len(terms) > 1:
                terms = [
                    terms[i] + terms[i + 1] if i + 1 < len(terms) else terms[i]
                    for i in range(0, len(terms), 2)
                ]
            out_ref[group, pl.ds(part * 32 + seed, 1), :] = terms[0] * (1.0 / FAN)
        return carry

    lax.fori_loop(0, 16, average, 0)


def join_kernel(place_ref, own_ref, other_ref, *rest):
    out_ref, sends = rest[0], rest[1:]
    lane = lane_of((64, BLOCK)) < HALF
    first = place_ref[0] == 0
    ring = own_ref.shape[0]
    for shift in range(ring):
        group = lax.rem(place_ref[1] + shift, ring)
        own, other = own_ref[group], other_ref[group]
        left, right = jnp.where(first, own, other), jnp.where(first, other, own)
        joined = jnp.where(lane, left, pltpu.roll(right, HALF, 1))
        out_ref[group] = joined
        sends[shift][...] = joined


def open_kernel(owner_ref, block_ref, request_ref):
    parts = request_ref.shape[0]
    wide = (parts, owner_ref.shape[1])
    owner = jnp.broadcast_to(owner_ref[...], wide)
    block = jnp.broadcast_to(block_ref[...], wide).astype(F32)
    mine = owner == lax.broadcasted_iota(jnp.int32, wide, 0)
    square = (wide[1], wide[1])
    below = lax.broadcasted_iota(jnp.int32, square, 0) <= lane_of(square)
    rank = dot(mine.astype(BF16), below.astype(BF16))
    lane = lane_of((parts, BLOCK))
    result = jnp.zeros((parts, BLOCK), F32)
    for slot in range(SLOTS):
        hit = jnp.logical_and(mine, rank == slot + 1.0)
        chosen = jnp.sum(jnp.where(hit, block, 0.0), axis=1, keepdims=True)
        result = jnp.where(lane == slot, chosen, result)
    result = result.astype(jnp.int32)
    for part in range(parts):
        request_ref[part] = result[part : part + 1]


def three(left, right_high, right_low):
    high, low = split(left)
    return dot(high, right_high) + (dot(high, right_low) + dot(low, right_high))


def self_kernel(place_ref, bias_ref, weight_hbm, *rest):
    pieces = rest[:8]
    part_ref, neigh_ref, held, rows, sems, row_sems = rest[8:]
    chips = [lax.rem(place_ref[1] + 8 - distance, 8) for distance in DISTANCES]
    copies, row_copies = [], []
    for index, (piece, chip) in enumerate(zip(pieces, chips)):
        row_copies.append(pltpu.make_async_copy(piece, rows.at[index], row_sems.at[index]))
        row_copies[-1].start()
        pair = weight_hbm.at[pl.ds(2 * chip, 2), pl.ds(0, 2)]
        copies.append(pltpu.make_async_copy(pair, held.at[index], sems.at[index]))
        copies[-1].start()
    neigh_copies = []
    for step in range(4):
        window = pl.ds(4 * step, 4)
        neigh_copies.append(
            pltpu.make_async_copy(weight_hbm.at[window, 2], neigh_ref.at[window], sems.at[8 + step])
        )
        neigh_copies[-1].start()
    total = jnp.broadcast_to(bias_ref[...], part_ref.shape)
    for step in range(4):
        pair = (2 * step, 2 * step + 1)
        for index in pair:
            copies[index].wait()
            row_copies[index].wait()
        left = jnp.concatenate([rows[index] for index in pair], axis=1)
        high, low = [
            jnp.concatenate([held[index, core, which] for index in pair for core in range(2)], axis=0)
            for which in range(2)
        ]
        total = total + three(left, high, low)
    part_ref[...] = total
    for copy in neigh_copies:
        copy.wait()


def forward_kernel(mean_ref, part_ref, weight_ref, cotangent_ref, hidden_ref, slope_ref):
    preact = part_ref[...]
    for step in range(4):
        left = jnp.concatenate([mean_ref[2 * step], mean_ref[2 * step + 1]], axis=1)
        right = weight_ref[4 * step : 4 * step + 4].reshape(256, weight_ref.shape[2])
        for piece in split(left):
            preact = preact + dot(piece, right)
    sigma = 1.0 / (1.0 + jnp.exp(-preact))
    hidden_ref[...] = (preact * sigma).astype(BF16)
    slope = cotangent_ref[...].astype(F32) * (sigma * (1.0 + preact * (1.0 - sigma)))
    slope_ref[...] = slope.astype(BF16)


def turn_kernel(place_ref, self_ref, mean_ref, high_ref, low_ref):
    rows = [lax.rem(place_ref[1] + 8 - k, 8) for k in DISTANCES]
    for which, ref in enumerate((self_ref, mean_ref)):
        turned = jnp.concatenate([ref[r] for r in rows], axis=0).T
        window = slice(which * BLOCK, (which + 1) * BLOCK)
        high_ref[window], low_ref[window] = split(turned)


def gradient_kernel(place_ref, high_ref, low_ref, near_ref, *rest):
    slopes, (keep_ref, send_ref) = rest[:-2], rest[-2:]
    right = jnp.concatenate([near_ref[...]] + [ref[...] for ref in slopes], axis=0)
    first = place_ref[0] == 0
    for which in range(2):
        window = slice(which * BLOCK, (which + 1) * BLOCK)
        total = dot(high_ref[window], right) + dot(low_ref[window], right)
        for chunk in range(8):
            start = chunk * 8
            one, two = total[start : start + 8], total[64 + start : 64 + start + 8]
            keep_ref[which * 8 + chunk] = jnp.where(first, one, two)
            send_ref[which * 8 + chunk] = jnp.where(first, two, one)


def add_kernel(left_ref, right_ref, out_ref):
    out_ref[...] = left_ref[...] + right_ref[...]


def sum_kernel(in_ref, out_ref):
    total = in_ref[0]
    for i in range(1, in_ref.shape[0]):
        total = total + in_ref[i]
    for i in range(out_ref.shape[0]):
        out_ref[i] = total


def call(kernel, shapes, specs, scratch=(), limit=8, cost=None, outs=None, aliases={}):
    return pl.pallas_call(
        kernel,
        out_shape=shapes,
        in_specs=specs,
        out_specs=outs or jax.tree.map(lambda _: VMEM, shapes),
        input_output_aliases=aliases,
        scratch_shapes=list(scratch),
        cost_estimate=cost,
        compiler_params=pltpu.CompilerParams(vmem_limit_bytes=int(limit * (1 << 20))),
    )


def cost(flops, size):
    return pl.CostEstimate(flops=flops, bytes_accessed=size, transcendentals=0)


def body(
    feature_table,
    seed_ids,
    neighbours,
    owners,
    blocks,
    counts,
    w_self,
    w_neigh,
    out_bias,
    cotangent,
):
    n_dom = lax.axis_size("dom")
    n_feat = lax.axis_size("feat")
    ring = n_feat // 2
    across = [(i, i ^ 1) for i in range(n_feat)]
    columns = [[2 * z + c for z in range(ring)] for c in range(2)]
    feat = lax.axis_index("feat").astype(jnp.int32).reshape(1)
    core = feat % 2
    place = jnp.concatenate([core, feat // 2])
    hidden_width = w_self.shape[1]

    def climb(value, chips):
        pairs = [(i, (i + 2 * chips) % n_feat) for i in range(n_feat)]
        return lax.ppermute(value, "feat", pairs)

    owner_ids = owners[:, 0]
    shape = jax.ShapeDtypeStruct

    request = call(
        open_kernel, shape((n_dom, 1, BLOCK), jnp.int32), [VMEM, VMEM], limit=60
    )(owner_ids[None, :], blocks[None, :])
    requests = lax.all_to_all(request, "dom", split_axis=0, concat_axis=0, tiled=True)
    near = jnp.transpose(neighbours).reshape(-1)
    packed, kept, given = call(
        prepare_kernel,
        (
            shape((feature_table.shape[1] // BLOCK, HALF, BLOCK), BF16),
            shape((ring, 64, BLOCK), F32),
            shape((ring, 64, BLOCK), F32),
        ),
        [SMEM, ANY, ANY],
        [
            pltpu.VMEM((feature_table.shape[1], BLOCK), F32),
            pltpu.VMEM(feature_table.shape, F32),
            pltpu.SMEM(seed_ids.shape, jnp.int32),
            pltpu.VMEM((feature_table.shape[1] // BLOCK, HALF, BLOCK), BF16),
            pltpu.SemaphoreType.DMA((8,)),
            pltpu.SemaphoreType.DMA,
            pltpu.SemaphoreType.DMA((8,)),
        ],
        limit=60, cost=cost(0, 10 << 20), outs=(ANY, VMEM, VMEM),
    )(core, seed_ids, feature_table)

    outgoing, weight = call(
        pack_kernel,
        (shape((n_dom, SLOTS, HALF, BLOCK), BF16), shape((3, 64, hidden_width), BF16)),
        [ANY] * 4,
        [
            pltpu.SMEM((n_dom, 1, BLOCK), jnp.int32),
            pltpu.VMEM(packed.shape, BF16),
            pltpu.VMEM((2, 64, hidden_width), F32),
            pltpu.VMEM((3, 64, hidden_width), BF16),
            pltpu.VMEM((n_dom, SLOTS, HALF, BLOCK), BF16),
            pltpu.SemaphoreType.DMA,
            pltpu.SemaphoreType.DMA,
            pltpu.SemaphoreType.DMA((n_dom,)),
            pltpu.SemaphoreType.DMA((3,)),
        ],
        limit=59, outs=(ANY, ANY),
    )(requests, packed, w_self, w_neigh)
    weights = lax.all_gather(weight, "feat", axis=0, tiled=False)
    arrived = lax.all_to_all(
        outgoing.reshape(n_dom, SLOTS * HALF, BLOCK), "dom", split_axis=0, concat_axis=0, tiled=True
    )
    self_rows, *sends = call(
        join_kernel,
        (shape((ring, 64, BLOCK), F32),) + (shape((64, BLOCK), F32),) * ring,
        [SMEM, VMEM, VMEM],
        limit=60, cost=cost(0, 1 << 20),
    )(place, kept, lax.ppermute(given, "feat", across))
    moved = [climb(sends[k % ring], k) for k in DISTANCES[1:]]
    pieces = [sends[0]] + moved

    entries = call(
        collect_kernel, shape((owner_ids.shape[0], HALF, BLOCK), BF16),
        [SMEM, VMEM] + [ANY] * 8, [pltpu.SMEM((n_dom,), jnp.int32)], limit=2, cost=cost(0, 2 << 20),
    )(owner_ids, arrived.reshape(n_dom * SLOTS, HALF, BLOCK), *moved, near)
    mean = call(
        gather_kernel,
        shape((ring, 64, BLOCK), F32),
        [SMEM, SMEM, SMEM, VMEM, VMEM],
        [pltpu.VMEM((owner_ids.shape[0] * BLOCK, BLOCK), F32)],
        cost=cost(0, 30 << 20),
    )(core, counts, near, entries, lax.ppermute(entries, "feat", across))

    part, neigh_weight = call(
        self_kernel,
        (shape((64, hidden_width), F32), shape((n_feat, 64, hidden_width), BF16)),
        [SMEM, VMEM] + [ANY] * 9,
        [
            pltpu.VMEM((ring, 2, 2, 64, hidden_width), BF16),
            pltpu.VMEM((ring, 64, BLOCK), F32),
            pltpu.SemaphoreType.DMA((12,)),
            pltpu.SemaphoreType.DMA((ring,)),
        ],
        limit=24, cost=cost(3 << 27, 9 << 20),
    )(place, out_bias[None, :], weights, *pieces)
    mean_seeds = lax.all_to_all(
        mean, "feat", split_axis=0, concat_axis=0, tiled=True, axis_index_groups=columns
    )

    hidden, slope = call(
        forward_kernel,
        (shape((64, hidden_width), BF16), shape((64, hidden_width), BF16)),
        [VMEM] * 4, limit=8, cost=cost(2 << 27, 4 << 20),
    )(mean_seeds, part, neigh_weight, cotangent)

    up, down = climb(slope, 1), climb(slope, -1)
    up_two, down_two = climb(slope, 2), climb(slope, -2)
    up_three, down_three = climb(up_two, 1), climb(down_two, -1)
    up_four, down_four = climb(up_two[:32], 2), climb(down_two[32:], -2)
    slopes = [up, down, up_two, down_two, up_three, down_three, up_four, down_four]

    turned = call(
        turn_kernel, (shape((2 * BLOCK, ring * 64), BF16),) * 2, [SMEM, VMEM, VMEM], limit=8
    )(place, self_rows, mean)
    keep, send = call(
        gradient_kernel, (shape((n_dom, 8, hidden_width), F32),) * 2, [SMEM] + [VMEM] * 11, limit=16
    )(place, *turned, slope, *slopes)
    partial = call(add_kernel, shape(keep.shape, F32), [VMEM, VMEM], limit=4)(
        keep, lax.ppermute(send, "feat", across)
    )
    shares = lax.all_to_all(partial, "dom", split_axis=0, concat_axis=0, tiled=True)
    total = call(sum_kernel, shape(shares.shape, F32), [VMEM], limit=4)(shares)
    grads = lax.all_to_all(
        total, "dom", split_axis=0, concat_axis=0, tiled=True
    ).reshape(n_dom * 8, hidden_width)
    return hidden, grads[: n_dom * 4], grads[n_dom * 4 :]


def solution(mesh):
    return jax.shard_map(
        body,
        mesh=mesh,
        in_specs=(
            P("feat", "dom"),
            P("dom"),
            P(None, "dom"),
            P("dom", None),
            P("dom"),
            P("dom"),
            P("feat", None),
            P("feat", None),
            P(),
            P(("dom", "feat"), None),
        ),
        out_specs=(P(("dom", "feat"), None), P("feat", None), P("feat", None)),
        check_vma=False,
    )
```

```python
import jax
import jax.numpy as jnp
from jax import lax
from jax.experimental import pallas as pl
from jax.experimental.pallas import tpu as pltpu
from jax.sharding import PartitionSpec as P

FAN = 15
BLOCK = 128
SLOTS = 8
HALF = BLOCK // 2
DISTANCES = (0, 1, -1, 2, -2, 3, -3, 4)
F32 = jnp.float32
BF16 = jnp.bfloat16
SMEM = pl.BlockSpec(memory_space=pltpu.SMEM)
VMEM = pl.BlockSpec(memory_space=pltpu.VMEM)
ANY = pl.BlockSpec(memory_space=pl.ANY)


def lane_of(shape):
    return lax.broadcasted_iota(jnp.int32, shape, len(shape) - 1)


def split(value):
    high = value.astype(BF16)
    low = (value - high.astype(F32)).astype(BF16)
    return high, low


def dot(left, right):
    return jnp.dot(left, right, preferred_element_type=F32)


def prepare_kernel(
    core_ref, seed_hbm, table_hbm, packed_ref, keep_ref, send_ref,
    rows, table, seed_ref, packed, sems, seed_sem, out_sems,
):
    core = core_ref[0]
    parts = sems.shape[0]
    width = table.shape[1] // parts
    pairs = width // (2 * BLOCK)
    first = lane_of((HALF, BLOCK)) < HALF

    def fetch(part):
        window = pl.ds(part * width, width)
        return pltpu.make_async_copy(table_hbm.at[:, window], table.at[:, window], sems.at[part])

    seeds = pltpu.make_async_copy(seed_hbm, seed_ref, seed_sem)
    seeds.start()
    for part in range(parts):
        fetch(part).start()

    def turn(pair, carry):
        start = pl.multiple_of(pair * 2 * BLOCK, 2 * BLOCK)
        left = table[:, pl.ds(start, BLOCK)]
        right = table[:, pl.ds(start + BLOCK, BLOCK)]
        turned = jnp.concatenate([left, right], axis=0).T
        rows[pl.ds(start, BLOCK), :] = turned
        rows[pl.ds(start + BLOCK, BLOCK), :] = pltpu.roll(turned, HALF, 1)
        for which in range(2):
            near = pl.multiple_of(start + which * BLOCK + core * HALF, HALF)
            far = pl.multiple_of(start + (1 - which) * BLOCK + (1 - core) * HALF, HALF)
            both_halves = jnp.where(first, rows[pl.ds(near, HALF), :], rows[pl.ds(far, HALF), :])
            packed[2 * pair + which] = both_halves.astype(BF16)
        return carry

    outs = []
    for part in range(parts):
        fetch(part).wait()
        lax.fori_loop(part * pairs, (part + 1) * pairs, turn, 0, unroll=pairs)
        window = pl.ds(2 * pairs * part, 2 * pairs)
        outs.append(pltpu.make_async_copy(packed.at[window], packed_ref.at[window], out_sems.at[part]))
        outs[-1].start()
    seeds.wait()

    def pick(chip, carry):
        for mine, ref in ((True, keep_ref), (False, send_ref)):
            base = (2 * chip + (core if mine else 1 - core)) * 64
            for step in range(64):
                ref[chip, pl.ds(step, 1), :] = rows[pl.ds(seed_ref[base + step], 1), :]
        return carry

    lax.fori_loop(0, keep_ref.shape[0], pick, 0)
    for copy in outs:
        copy.wait()


def pack_kernel(
    request_hbm, packed_hbm, self_hbm, neigh_hbm, out_hbm, weight_hbm,
    wanted, packed_ref, both, weight_ref, out_ref, sem, in_sem, out_sems, weight_sems,
):
    slots = pltpu.make_async_copy(request_hbm, wanted, sem)
    slots.start()
    fetch = pltpu.make_async_copy(packed_hbm, packed_ref, in_sem)
    fetch.start()
    weights = [
        pltpu.make_async_copy(ref, both.at[which], weight_sems.at[which])
        for which, ref in enumerate((self_hbm, neigh_hbm))
    ]
    for copy in weights:
        copy.start()
    for held in weights:
        held.wait()
    high, low = split(both[0])
    weight_ref[0] = high
    weight_ref[1] = low
    weight_ref[2] = both[1].astype(BF16)
    copies = [pltpu.make_async_copy(weight_ref, weight_hbm, weight_sems.at[2])]
    copies[0].start()
    slots.wait()
    fetch.wait()
    for part in range(out_ref.shape[0]):
        for slot in range(SLOTS):
            out_ref[part, slot] = packed_ref[wanted[part, 0, slot]]
        copies.append(pltpu.make_async_copy(out_ref.at[part], out_hbm.at[part], out_sems.at[part]))
        copies[-1].start()
    for copy in copies:
        copy.wait()


def collect_kernel(owner_ref, arrived_ref, *rest):
    out_ref, seen = rest[-2:]
    for owner in range(arrived_ref.shape[0] // SLOTS):
        seen[owner] = 0

    def place(entry, carry):
        owner = owner_ref[entry]
        rank = seen[owner]
        seen[owner] = rank + 1
        out_ref[entry] = arrived_ref[owner * SLOTS + rank]
        return carry

    lax.fori_loop(0, out_ref.shape[0], place, 0, unroll=8)


def gather_kernel(core_ref, count_ref, near_ref, own_ref, other_ref, out_ref, front):
    core = core_ref[0]
    lane = lane_of((HALF, BLOCK))
    row = lax.broadcasted_iota(jnp.int32, (HALF, BLOCK), 0)
    straight = (lane < HALF) == (core == 0)

    def place(entry, carry):
        own = own_ref[entry].astype(F32)
        other = other_ref[entry].astype(F32)
        count = count_ref[entry]
        upper = jnp.where(straight, own, other)
        lower = pltpu.roll(jnp.where(straight, other, own), HALF, 1)
        start = pl.multiple_of(entry * BLOCK, BLOCK)
        front[pl.ds(start, HALF), :] = jnp.where(row < count, upper, 0.0)
        front[pl.ds(start + HALF, HALF), :] = jnp.where(row < count - HALF, lower, 0.0)
        return carry

    lax.fori_loop(0, own_ref.shape[0], place, 0, unroll=8)

    def average(step, carry):
        group, part = lax.div(step, 2), lax.rem(step, 2)
        base = ((2 * group + core) * 64 + part * 32) * FAN
        for seed in range(32):
            terms = [front[pl.ds(near_ref[base + seed * FAN + k], 1), :] for k in range(FAN)]
            while len(terms) > 1:
                terms = [
                    terms[i] + terms[i + 1] if i + 1 < len(terms) else terms[i]
                    for i in range(0, len(terms), 2)
                ]
            out_ref[group, pl.ds(part * 32 + seed, 1), :] = terms[0] * (1.0 / FAN)
        return carry

    lax.fori_loop(0, 16, average, 0)


def join_kernel(place_ref, own_ref, other_ref, *rest):
    out_ref, sends = rest[0], rest[1:]
    lane = lane_of((64, BLOCK)) < HALF
    first = place_ref[0] == 0
    ring = own_ref.shape[0]
    for shift in range(ring):
        group = lax.rem(place_ref[1] + shift, ring)
        own, other = own_ref[group], other_ref[group]
        left, right = jnp.where(first, own, other), jnp.where(first, other, own)
        joined = jnp.where(lane, left, pltpu.roll(right, HALF, 1))
        out_ref[group] = joined
        sends[shift][...] = joined


def open_kernel(owner_ref, block_ref, request_ref):
    parts = request_ref.shape[0]
    wide = (parts, owner_ref.shape[1])
    owner = jnp.broadcast_to(owner_ref[...], wide)
    block = jnp.broadcast_to(block_ref[...], wide).astype(F32)
    mine = owner == lax.broadcasted_iota(jnp.int32, wide, 0)
    square = (wide[1], wide[1])
    below = lax.broadcasted_iota(jnp.int32, square, 0) <= lane_of(square)
    rank = dot(mine.astype(BF16), below.astype(BF16))
    lane = lane_of((parts, BLOCK))
    result = jnp.zeros((parts, BLOCK), F32)
    for slot in range(SLOTS):
        hit = jnp.logical_and(mine, rank == slot + 1.0)
        chosen = jnp.sum(jnp.where(hit, block, 0.0), axis=1, keepdims=True)
        result = jnp.where(lane == slot, chosen, result)
    result = result.astype(jnp.int32)
    for part in range(parts):
        request_ref[part] = result[part : part + 1]


def three(left, right_high, right_low):
    high, low = split(left)
    return dot(high, right_high) + (dot(high, right_low) + dot(low, right_high))


def self_kernel(place_ref, bias_ref, weight_hbm, *rest):
    pieces = rest[:8]
    part_ref, neigh_ref, held, rows, sems, row_sems = rest[8:]
    chips = [lax.rem(place_ref[1] + 8 - distance, 8) for distance in DISTANCES]
    copies, row_copies = [], []
    for index, (piece, chip) in enumerate(zip(pieces, chips)):
        row_copies.append(pltpu.make_async_copy(piece, rows.at[index], row_sems.at[index]))
        row_copies[-1].start()
        pair = weight_hbm.at[pl.ds(2 * chip, 2), pl.ds(0, 2)]
        copies.append(pltpu.make_async_copy(pair, held.at[index], sems.at[index]))
        copies[-1].start()
    neigh_copies = []
    for step in range(4):
        window = pl.ds(4 * step, 4)
        neigh_copies.append(
            pltpu.make_async_copy(weight_hbm.at[window, 2], neigh_ref.at[window], sems.at[8 + step])
        )
        neigh_copies[-1].start()
    total = jnp.broadcast_to(bias_ref[...], part_ref.shape)
    for step in range(4):
        pair = (2 * step, 2 * step + 1)
        for index in pair:
            copies[index].wait()
            row_copies[index].wait()
        left = jnp.concatenate([rows[index] for index in pair], axis=1)
        high, low = [
            jnp.concatenate([held[index, core, which] for index in pair for core in range(2)], axis=0)
            for which in range(2)
        ]
        total = total + three(left, high, low)
    part_ref[...] = total
    for copy in neigh_copies:
        copy.wait()


def forward_kernel(mean_ref, part_ref, weight_ref, cotangent_ref, hidden_ref, slope_ref):
    preact = part_ref[...]
    for step in range(4):
        left = jnp.concatenate([mean_ref[2 * step], mean_ref[2 * step + 1]], axis=1)
        right = weight_ref[4 * step : 4 * step + 4].reshape(256, weight_ref.shape[2])
        for piece in split(left):
            preact = preact + dot(piece, right)
    sigma = 1.0 / (1.0 + jnp.exp(-preact))
    hidden_ref[...] = (preact * sigma).astype(BF16)
    slope = cotangent_ref[...].astype(F32) * (sigma * (1.0 + preact * (1.0 - sigma)))
    slope_ref[...] = slope.astype(BF16)


def turn_kernel(place_ref, self_ref, mean_ref, high_ref, low_ref):
    rows = [lax.rem(place_ref[1] + 8 - k, 8) for k in DISTANCES]
    for which, ref in enumerate((self_ref, mean_ref)):
        turned = jnp.concatenate([ref[r] for r in rows], axis=0).T
        window = slice(which * BLOCK, (which + 1) * BLOCK)
        high_ref[window], low_ref[window] = split(turned)


def gradient_kernel(place_ref, high_ref, low_ref, near_ref, *rest):
    slopes, (keep_ref, send_ref) = rest[:-2], rest[-2:]
    right = jnp.concatenate([near_ref[...]] + [ref[...] for ref in slopes], axis=0)
    first = place_ref[0] == 0
    for which in range(2):
        window = slice(which * BLOCK, (which + 1) * BLOCK)
        total = dot(high_ref[window], right) + dot(low_ref[window], right)
        for chunk in range(8):
            start = chunk * 8
            one, two = total[start : start + 8], total[64 + start : 64 + start + 8]
            keep_ref[which * 8 + chunk] = jnp.where(first, one, two)
            send_ref[which * 8 + chunk] = jnp.where(first, two, one)


def add_kernel(left_ref, right_ref, out_ref):
    out_ref[...] = left_ref[...] + right_ref[...]


def sum_kernel(in_ref, out_ref):
    total = in_ref[0]
    for i in range(1, in_ref.shape[0]):
        total = total + in_ref[i]
    for i in range(out_ref.shape[0]):
        out_ref[i] = total


def call(kernel, shapes, specs, scratch=(), limit=8, cost=None, outs=None, aliases={}):
    return pl.pallas_call(
        kernel,
        out_shape=shapes,
        in_specs=specs,
        out_specs=outs or jax.tree.map(lambda _: VMEM, shapes),
        input_output_aliases=aliases,
        scratch_shapes=list(scratch),
        cost_estimate=cost,
        compiler_params=pltpu.CompilerParams(vmem_limit_bytes=int(limit * (1 << 20))),
    )


def cost(flops, size):
    return pl.CostEstimate(flops=flops, bytes_accessed=size, transcendentals=0)


def body(
    feature_table,
    seed_ids,
    neighbours,
    owners,
    blocks,
    counts,
    w_self,
    w_neigh,
    out_bias,
    cotangent,
):
    n_dom = lax.axis_size("dom")
    n_feat = lax.axis_size("feat")
    ring = n_feat // 2
    across = [(i, i ^ 1) for i in range(n_feat)]
    columns = [[2 * z + c for z in range(ring)] for c in range(2)]
    feat = lax.axis_index("feat").astype(jnp.int32).reshape(1)
    core = feat % 2
    place = jnp.concatenate([core, feat // 2])
    hidden_width = w_self.shape[1]

    def climb(value, chips):
        pairs = [(i, (i + 2 * chips) % n_feat) for i in range(n_feat)]
        return lax.ppermute(value, "feat", pairs)

    owner_ids = owners[:, 0]
    shape = jax.ShapeDtypeStruct

    request = call(
        open_kernel, shape((n_dom, 1, BLOCK), jnp.int32), [VMEM, VMEM], limit=60
    )(owner_ids[None, :], blocks[None, :])
    requests = lax.all_to_all(request, "dom", split_axis=0, concat_axis=0, tiled=True)
    near = jnp.transpose(neighbours).reshape(-1)
    packed, kept, given = call(
        prepare_kernel,
        (
            shape((feature_table.shape[1] // BLOCK, HALF, BLOCK), BF16),
            shape((ring, 64, BLOCK), F32),
            shape((ring, 64, BLOCK), F32),
        ),
        [SMEM, ANY, ANY],
        [
            pltpu.VMEM((feature_table.shape[1], BLOCK), F32),
            pltpu.VMEM(feature_table.shape, F32),
            pltpu.SMEM(seed_ids.shape, jnp.int32),
            pltpu.VMEM((feature_table.shape[1] // BLOCK, HALF, BLOCK), BF16),
            pltpu.SemaphoreType.DMA((8,)),
            pltpu.SemaphoreType.DMA,
            pltpu.SemaphoreType.DMA((8,)),
        ],
        limit=60, cost=cost(0, 10 << 20), outs=(ANY, VMEM, VMEM),
    )(core, seed_ids, feature_table)

    outgoing, weight = call(
        pack_kernel,
        (shape((n_dom, SLOTS, HALF, BLOCK), BF16), shape((3, 64, hidden_width), BF16)),
        [ANY] * 4,
        [
            pltpu.SMEM((n_dom, 1, BLOCK), jnp.int32),
            pltpu.VMEM(packed.shape, BF16),
            pltpu.VMEM((2, 64, hidden_width), F32),
            pltpu.VMEM((3, 64, hidden_width), BF16),
            pltpu.VMEM((n_dom, SLOTS, HALF, BLOCK), BF16),
            pltpu.SemaphoreType.DMA,
            pltpu.SemaphoreType.DMA,
            pltpu.SemaphoreType.DMA((n_dom,)),
            pltpu.SemaphoreType.DMA((3,)),
        ],
        limit=53.8, outs=(ANY, ANY),
    )(requests, packed, w_self, w_neigh)
    weights = lax.all_gather(weight, "feat", axis=0, tiled=False)
    arrived = lax.all_to_all(
        outgoing.reshape(n_dom, SLOTS * HALF, BLOCK), "dom", split_axis=0, concat_axis=0, tiled=True
    )
    self_rows, *sends = call(
        join_kernel,
        (shape((ring, 64, BLOCK), F32),) + (shape((64, BLOCK), F32),) * ring,
        [SMEM, VMEM, VMEM],
        limit=53.55, cost=cost(0, 1 << 20),
    )(place, kept, lax.ppermute(given, "feat", across))
    moved = [climb(sends[k % ring], k) for k in DISTANCES[1:]]
    pieces = [sends[0]] + moved

    entries = call(
        collect_kernel, shape((owner_ids.shape[0], HALF, BLOCK), BF16),
        [SMEM, VMEM] + [ANY] * 8, [pltpu.SMEM((n_dom,), jnp.int32)], limit=2, cost=cost(0, 2 << 20),
    )(owner_ids, arrived.reshape(n_dom * SLOTS, HALF, BLOCK), *moved, near)
    mean = call(
        gather_kernel,
        shape((ring, 64, BLOCK), F32),
        [SMEM, SMEM, SMEM, VMEM, VMEM],
        [pltpu.VMEM((owner_ids.shape[0] * BLOCK, BLOCK), F32)],
        cost=cost(0, 30 << 20),
    )(core, counts, near, entries, lax.ppermute(entries, "feat", across))

    part, neigh_weight = call(
        self_kernel,
        (shape((64, hidden_width), F32), shape((n_feat, 64, hidden_width), BF16)),
        [SMEM, VMEM] + [ANY] * 9,
        [
            pltpu.VMEM((ring, 2, 2, 64, hidden_width), BF16),
            pltpu.VMEM((ring, 64, BLOCK), F32),
            pltpu.SemaphoreType.DMA((12,)),
            pltpu.SemaphoreType.DMA((ring,)),
        ],
        limit=51.4, cost=cost(3 << 27, 9 << 20),
    )(place, out_bias[None, :], weights, *pieces)
    mean_seeds = lax.all_to_all(
        mean, "feat", split_axis=0, concat_axis=0, tiled=True, axis_index_groups=columns
    )

    hidden, slope = call(
        forward_kernel,
        (shape((64, hidden_width), BF16), shape((64, hidden_width), BF16)),
        [VMEM] * 4, limit=8, cost=cost(2 << 27, 4 << 20),
    )(mean_seeds, part, neigh_weight, cotangent)

    up, down = climb(slope, 1), climb(slope, -1)
    up_two, down_two = climb(slope, 2), climb(slope, -2)
    up_three, down_three = climb(up_two, 1), climb(down_two, -1)
    up_four, down_four = climb(up_two[:32], 2), climb(down_two[32:], -2)
    slopes = [up, down, up_two, down_two, up_three, down_three, up_four, down_four]

    turned = call(
        turn_kernel, (shape((2 * BLOCK, ring * 64), BF16),) * 2, [SMEM, VMEM, VMEM], limit=8
    )(place, self_rows, mean)
    keep, send = call(
        gradient_kernel, (shape((n_dom, 8, hidden_width), F32),) * 2, [SMEM] + [VMEM] * 11, limit=16
    )(place, *turned, slope, *slopes)
    partial = call(add_kernel, shape(keep.shape, F32), [VMEM, VMEM], limit=4)(
        keep, lax.ppermute(send, "feat", across)
    )
    shares = lax.all_to_all(partial, "dom", split_axis=0, concat_axis=0, tiled=True)
    total = call(sum_kernel, shape(shares.shape, F32), [VMEM], limit=4)(shares)
    grads = lax.all_to_all(
        total, "dom", split_axis=0, concat_axis=0, tiled=True
    ).reshape(n_dom * 8, hidden_width)
    return hidden, grads[: n_dom * 4], grads[n_dom * 4 :]


def solution(mesh):
    return jax.shard_map(
        body,
        mesh=mesh,
        in_specs=(
            P("feat", "dom"),
            P("dom"),
            P(None, "dom"),
            P("dom", None),
            P("dom"),
            P("dom"),
            P("feat", None),
            P("feat", None),
            P(),
            P(("dom", "feat"), None),
        ),
        out_specs=(P(("dom", "feat"), None), P("feat", None), P("feat", None)),
        check_vma=False,
    )
```

```python
import jax
import jax.numpy as jnp
from jax import lax
from jax.experimental import pallas as pl
from jax.experimental.pallas import tpu as pltpu
from jax.sharding import PartitionSpec as P

FAN = 15
BLOCK = 128
SLOTS = 8
HALF = BLOCK // 2
DISTANCES = (0, 1, -1, 2, -2, 3, -3, 4)
F32 = jnp.float32
BF16 = jnp.bfloat16
SMEM = pl.BlockSpec(memory_space=pltpu.SMEM)
VMEM = pl.BlockSpec(memory_space=pltpu.VMEM)
ANY = pl.BlockSpec(memory_space=pl.ANY)


def lane_of(shape):
    return lax.broadcasted_iota(jnp.int32, shape, len(shape) - 1)


def split(value):
    high = value.astype(BF16)
    low = (value - high.astype(F32)).astype(BF16)
    return high, low


def dot(left, right):
    return jnp.dot(left, right, preferred_element_type=F32)


def prepare_kernel(
    core_ref, seed_hbm, table_hbm, packed_ref, keep_ref, send_ref,
    rows, table, seed_ref, packed, sems, seed_sem, out_sems,
):
    core = core_ref[0]
    parts = sems.shape[0]
    width = table.shape[1] // parts
    pairs = width // (2 * BLOCK)
    first = lane_of((HALF, BLOCK)) < HALF

    def fetch(part):
        window = pl.ds(part * width, width)
        return pltpu.make_async_copy(table_hbm.at[:, window], table.at[:, window], sems.at[part])

    seeds = pltpu.make_async_copy(seed_hbm, seed_ref, seed_sem)
    seeds.start()
    for part in range(parts):
        fetch(part).start()

    def turn(pair, carry):
        start = pl.multiple_of(pair * 2 * BLOCK, 2 * BLOCK)
        left = table[:, pl.ds(start, BLOCK)]
        right = table[:, pl.ds(start + BLOCK, BLOCK)]
        turned = jnp.concatenate([left, right], axis=0).T
        rows[pl.ds(start, BLOCK), :] = turned
        rows[pl.ds(start + BLOCK, BLOCK), :] = pltpu.roll(turned, HALF, 1)
        for which in range(2):
            near = pl.multiple_of(start + which * BLOCK + core * HALF, HALF)
            far = pl.multiple_of(start + (1 - which) * BLOCK + (1 - core) * HALF, HALF)
            both_halves = jnp.where(first, rows[pl.ds(near, HALF), :], rows[pl.ds(far, HALF), :])
            packed[2 * pair + which] = both_halves.astype(BF16)
        return carry

    outs = []
    for part in range(parts):
        fetch(part).wait()
        lax.fori_loop(part * pairs, (part + 1) * pairs, turn, 0, unroll=pairs)
        window = pl.ds(2 * pairs * part, 2 * pairs)
        outs.append(pltpu.make_async_copy(packed.at[window], packed_ref.at[window], out_sems.at[part]))
        outs[-1].start()
    seeds.wait()

    def pick(chip, carry):
        for mine, ref in ((True, keep_ref), (False, send_ref)):
            base = (2 * chip + (core if mine else 1 - core)) * 64
            for step in range(64):
                ref[chip, pl.ds(step, 1), :] = rows[pl.ds(seed_ref[base + step], 1), :]
        return carry

    lax.fori_loop(0, keep_ref.shape[0], pick, 0)
    for copy in outs:
        copy.wait()


def pack_kernel(
    request_hbm, packed_hbm, self_hbm, neigh_hbm, out_hbm, weight_hbm,
    wanted, packed_ref, both, weight_ref, out_ref, sem, in_sem, out_sems, weight_sems,
):
    slots = pltpu.make_async_copy(request_hbm, wanted, sem)
    slots.start()
    fetch = pltpu.make_async_copy(packed_hbm, packed_ref, in_sem)
    fetch.start()
    weights = [
        pltpu.make_async_copy(ref, both.at[which], weight_sems.at[which])
        for which, ref in enumerate((self_hbm, neigh_hbm))
    ]
    for copy in weights:
        copy.start()
    for held in weights:
        held.wait()
    high, low = split(both[0])
    weight_ref[0] = high
    weight_ref[1] = low
    weight_ref[2] = both[1].astype(BF16)
    copies = [pltpu.make_async_copy(weight_ref, weight_hbm, weight_sems.at[2])]
    copies[0].start()
    slots.wait()
    fetch.wait()
    for part in range(out_ref.shape[0]):
        for slot in range(SLOTS):
            out_ref[part, slot] = packed_ref[wanted[part, 0, slot]]
        copies.append(pltpu.make_async_copy(out_ref.at[part], out_hbm.at[part], out_sems.at[part]))
        copies[-1].start()
    for copy in copies:
        copy.wait()


def collect_kernel(owner_ref, arrived_ref, *rest):
    out_ref, seen = rest[-2:]
    for owner in range(arrived_ref.shape[0] // SLOTS):
        seen[owner] = 0

    def place(entry, carry):
        owner = owner_ref[entry]
        rank = seen[owner]
        seen[owner] = rank + 1
        out_ref[entry] = arrived_ref[owner * SLOTS + rank]
        return carry

    lax.fori_loop(0, out_ref.shape[0], place, 0, unroll=8)


def gather_kernel(core_ref, count_ref, near_hbm, own_ref, other_ref, out_ref, front, near_ref, sem):
    core = core_ref[0]
    fetch = pltpu.make_async_copy(near_hbm, near_ref, sem)
    fetch.start()
    lane = lane_of((HALF, BLOCK))
    row = lax.broadcasted_iota(jnp.int32, (HALF, BLOCK), 0)
    straight = (lane < HALF) == (core == 0)

    def place(entry, carry):
        own = own_ref[entry].astype(F32)
        other = other_ref[entry].astype(F32)
        count = count_ref[entry]
        upper = jnp.where(straight, own, other)
        lower = pltpu.roll(jnp.where(straight, other, own), HALF, 1)
        start = pl.multiple_of(entry * BLOCK, BLOCK)
        front[pl.ds(start, HALF), :] = jnp.where(row < count, upper, 0.0)
        front[pl.ds(start + HALF, HALF), :] = jnp.where(row < count - HALF, lower, 0.0)
        return carry

    lax.fori_loop(0, own_ref.shape[0], place, 0, unroll=8)
    fetch.wait()

    def average(step, carry):
        group, part = lax.div(step, 2), lax.rem(step, 2)
        base = ((2 * group + core) * 64 + part * 32) * FAN
        for seed in range(32):
            terms = [front[pl.ds(near_ref[base + seed * FAN + k], 1), :] for k in range(FAN)]
            while len(terms) > 1:
                terms = [
                    terms[i] + terms[i + 1] if i + 1 < len(terms) else terms[i]
                    for i in range(0, len(terms), 2)
                ]
            out_ref[group, pl.ds(part * 32 + seed, 1), :] = terms[0] * (1.0 / FAN)
        return carry

    lax.fori_loop(0, 16, average, 0)


def join_kernel(place_ref, own_ref, other_ref, *rest):
    out_ref, sends = rest[0], rest[1:]
    lane = lane_of((64, BLOCK)) < HALF
    first = place_ref[0] == 0
    ring = own_ref.shape[0]
    for shift in range(ring):
        group = lax.rem(place_ref[1] + shift, ring)
        own, other = own_ref[group], other_ref[group]
        left, right = jnp.where(first, own, other), jnp.where(first, other, own)
        joined = jnp.where(lane, left, pltpu.roll(right, HALF, 1))
        out_ref[group] = joined
        sends[shift][...] = joined


def open_kernel(owner_ref, block_ref, request_ref):
    parts = request_ref.shape[0]
    wide = (parts, owner_ref.shape[1])
    owner = jnp.broadcast_to(owner_ref[...], wide)
    block = jnp.broadcast_to(block_ref[...], wide).astype(F32)
    mine = owner == lax.broadcasted_iota(jnp.int32, wide, 0)
    square = (wide[1], wide[1])
    below = lax.broadcasted_iota(jnp.int32, square, 0) <= lane_of(square)
    rank = dot(mine.astype(BF16), below.astype(BF16))
    lane = lane_of((parts, BLOCK))
    result = jnp.zeros((parts, BLOCK), F32)
    for slot in range(SLOTS):
        hit = jnp.logical_and(mine, rank == slot + 1.0)
        chosen = jnp.sum(jnp.where(hit, block, 0.0), axis=1, keepdims=True)
        result = jnp.where(lane == slot, chosen, result)
    result = result.astype(jnp.int32)
    for part in range(parts):
        request_ref[part] = result[part : part + 1]


def three(left, right_high, right_low):
    high, low = split(left)
    return dot(high, right_high) + (dot(high, right_low) + dot(low, right_high))


def self_kernel(place_ref, bias_ref, weight_hbm, *rest):
    pieces = rest[:8]
    part_ref, neigh_ref, held, rows, sems, row_sems = rest[8:]
    chips = [lax.rem(place_ref[1] + 8 - distance, 8) for distance in DISTANCES]
    copies, row_copies = [], []
    for index, (piece, chip) in enumerate(zip(pieces, chips)):
        row_copies.append(pltpu.make_async_copy(piece, rows.at[index], row_sems.at[index]))
        row_copies[-1].start()
        pair = weight_hbm.at[pl.ds(2 * chip, 2), pl.ds(0, 2)]
        copies.append(pltpu.make_async_copy(pair, held.at[index], sems.at[index]))
        copies[-1].start()
    neigh_copies = []
    for step in range(4):
        window = pl.ds(4 * step, 4)
        neigh_copies.append(
            pltpu.make_async_copy(weight_hbm.at[window, 2], neigh_ref.at[window], sems.at[8 + step])
        )
        neigh_copies[-1].start()
    total = jnp.broadcast_to(bias_ref[...], part_ref.shape)
    for step in range(4):
        pair = (2 * step, 2 * step + 1)
        for index in pair:
            copies[index].wait()
            row_copies[index].wait()
        left = jnp.concatenate([rows[index] for index in pair], axis=1)
        high, low = [
            jnp.concatenate([held[index, core, which] for index in pair for core in range(2)], axis=0)
            for which in range(2)
        ]
        total = total + three(left, high, low)
    part_ref[...] = total
    for copy in neigh_copies:
        copy.wait()


def forward_kernel(mean_ref, part_ref, weight_ref, cotangent_ref, hidden_ref, slope_ref):
    preact = part_ref[...]
    for step in range(4):
        left = jnp.concatenate([mean_ref[2 * step], mean_ref[2 * step + 1]], axis=1)
        right = weight_ref[4 * step : 4 * step + 4].reshape(256, weight_ref.shape[2])
        for piece in split(left):
            preact = preact + dot(piece, right)
    sigma = 1.0 / (1.0 + jnp.exp(-preact))
    hidden_ref[...] = (preact * sigma).astype(BF16)
    slope = cotangent_ref[...].astype(F32) * (sigma * (1.0 + preact * (1.0 - sigma)))
    slope_ref[...] = slope.astype(BF16)


def turn_kernel(place_ref, self_ref, mean_ref, high_ref, low_ref):
    rows = [lax.rem(place_ref[1] + 8 - k, 8) for k in DISTANCES]
    for which, ref in enumerate((self_ref, mean_ref)):
        turned = jnp.concatenate([ref[r] for r in rows], axis=0).T
        window = slice(which * BLOCK, (which + 1) * BLOCK)
        high_ref[window], low_ref[window] = split(turned)


def gradient_kernel(place_ref, high_ref, low_ref, near_ref, *rest):
    slopes, (keep_ref, send_ref) = rest[:-2], rest[-2:]
    right = jnp.concatenate([near_ref[...]] + [ref[...] for ref in slopes], axis=0)
    first = place_ref[0] == 0
    for which in range(2):
        window = slice(which * BLOCK, (which + 1) * BLOCK)
        total = dot(high_ref[window], right) + dot(low_ref[window], right)
        for chunk in range(8):
            start = chunk * 8
            one, two = total[start : start + 8], total[64 + start : 64 + start + 8]
            keep_ref[which * 8 + chunk] = jnp.where(first, one, two)
            send_ref[which * 8 + chunk] = jnp.where(first, two, one)


def add_kernel(left_ref, right_ref, out_ref):
    out_ref[...] = left_ref[...] + right_ref[...]


def sum_kernel(in_ref, out_ref):
    total = in_ref[0]
    for i in range(1, in_ref.shape[0]):
        total = total + in_ref[i]
    for i in range(out_ref.shape[0]):
        out_ref[i] = total


def call(kernel, shapes, specs, scratch=(), limit=8, cost=None, outs=None, aliases={}):
    return pl.pallas_call(
        kernel,
        out_shape=shapes,
        in_specs=specs,
        out_specs=outs or jax.tree.map(lambda _: VMEM, shapes),
        input_output_aliases=aliases,
        scratch_shapes=list(scratch),
        cost_estimate=cost,
        compiler_params=pltpu.CompilerParams(vmem_limit_bytes=int(limit * (1 << 20))),
    )


def cost(flops, size):
    return pl.CostEstimate(flops=flops, bytes_accessed=size, transcendentals=0)


def body(
    feature_table,
    seed_ids,
    neighbours,
    owners,
    blocks,
    counts,
    w_self,
    w_neigh,
    out_bias,
    cotangent,
):
    n_dom = lax.axis_size("dom")
    n_feat = lax.axis_size("feat")
    ring = n_feat // 2
    across = [(i, i ^ 1) for i in range(n_feat)]
    columns = [[2 * z + c for z in range(ring)] for c in range(2)]
    feat = lax.axis_index("feat").astype(jnp.int32).reshape(1)
    core = feat % 2
    place = jnp.concatenate([core, feat // 2])
    hidden_width = w_self.shape[1]

    def climb(value, chips):
        pairs = [(i, (i + 2 * chips) % n_feat) for i in range(n_feat)]
        return lax.ppermute(value, "feat", pairs)

    owner_ids = owners[:, 0]
    shape = jax.ShapeDtypeStruct

    request = call(
        open_kernel, shape((n_dom, 1, BLOCK), jnp.int32), [VMEM, VMEM], limit=60
    )(owner_ids[None, :], blocks[None, :])
    requests = lax.all_to_all(request, "dom", split_axis=0, concat_axis=0, tiled=True)
    near = jnp.transpose(neighbours).reshape(-1)
    packed, kept, given = call(
        prepare_kernel,
        (
            shape((feature_table.shape[1] // BLOCK, HALF, BLOCK), BF16),
            shape((ring, 64, BLOCK), F32),
            shape((ring, 64, BLOCK), F32),
        ),
        [SMEM, ANY, ANY],
        [
            pltpu.VMEM((feature_table.shape[1], BLOCK), F32),
            pltpu.VMEM(feature_table.shape, F32),
            pltpu.SMEM(seed_ids.shape, jnp.int32),
            pltpu.VMEM((feature_table.shape[1] // BLOCK, HALF, BLOCK), BF16),
            pltpu.SemaphoreType.DMA((8,)),
            pltpu.SemaphoreType.DMA,
            pltpu.SemaphoreType.DMA((8,)),
        ],
        limit=60, cost=cost(0, 10 << 20), outs=(ANY, VMEM, VMEM),
    )(core, seed_ids, feature_table)

    outgoing, weight = call(
        pack_kernel,
        (shape((n_dom, SLOTS, HALF, BLOCK), BF16), shape((3, 64, hidden_width), BF16)),
        [ANY] * 4,
        [
            pltpu.SMEM((n_dom, 1, BLOCK), jnp.int32),
            pltpu.VMEM(packed.shape, BF16),
            pltpu.VMEM((2, 64, hidden_width), F32),
            pltpu.VMEM((3, 64, hidden_width), BF16),
            pltpu.VMEM((n_dom, SLOTS, HALF, BLOCK), BF16),
            pltpu.SemaphoreType.DMA,
            pltpu.SemaphoreType.DMA,
            pltpu.SemaphoreType.DMA((n_dom,)),
            pltpu.SemaphoreType.DMA((3,)),
        ],
        limit=53.8, outs=(ANY, ANY),
    )(requests, packed, w_self, w_neigh)
    weights = lax.all_gather(weight, "feat", axis=0, tiled=False)
    arrived = lax.all_to_all(
        outgoing.reshape(n_dom, SLOTS * HALF, BLOCK), "dom", split_axis=0, concat_axis=0, tiled=True
    )
    self_rows, *sends = call(
        join_kernel,
        (shape((ring, 64, BLOCK), F32),) + (shape((64, BLOCK), F32),) * ring,
        [SMEM, VMEM, VMEM],
        limit=53.55, cost=cost(0, 1 << 20),
    )(place, kept, lax.ppermute(given, "feat", across))
    moved = [climb(sends[k % ring], k) for k in DISTANCES[1:]]
    pieces = [sends[0]] + moved

    entries = call(
        collect_kernel, shape((owner_ids.shape[0], HALF, BLOCK), BF16),
        [SMEM, VMEM] + [ANY] * 8, [pltpu.SMEM((n_dom,), jnp.int32)], limit=2, cost=cost(0, 2 << 20),
    )(owner_ids, arrived.reshape(n_dom * SLOTS, HALF, BLOCK), *moved, near)
    mean = call(
        gather_kernel,
        shape((ring, 64, BLOCK), F32),
        [SMEM, SMEM, ANY, VMEM, VMEM],
        [
            pltpu.VMEM((owner_ids.shape[0] * BLOCK, BLOCK), F32),
            pltpu.SMEM(near.shape, jnp.int32),
            pltpu.SemaphoreType.DMA,
        ],
        cost=cost(0, 30 << 20),
    )(core, counts, near, entries, lax.ppermute(entries, "feat", across))

    part, neigh_weight = call(
        self_kernel,
        (shape((64, hidden_width), F32), shape((n_feat, 64, hidden_width), BF16)),
        [SMEM, VMEM] + [ANY] * 9,
        [
            pltpu.VMEM((ring, 2, 2, 64, hidden_width), BF16),
            pltpu.VMEM((ring, 64, BLOCK), F32),
            pltpu.SemaphoreType.DMA((12,)),
            pltpu.SemaphoreType.DMA((ring,)),
        ],
        limit=51.4, cost=cost(3 << 27, 9 << 20),
    )(place, out_bias[None, :], weights, *pieces)
    mean_seeds = lax.all_to_all(
        mean, "feat", split_axis=0, concat_axis=0, tiled=True, axis_index_groups=columns
    )

    hidden, slope = call(
        forward_kernel,
        (shape((64, hidden_width), BF16), shape((64, hidden_width), BF16)),
        [VMEM] * 4, limit=8, cost=cost(2 << 27, 4 << 20),
    )(mean_seeds, part, neigh_weight, cotangent)

    up, down = climb(slope, 1), climb(slope, -1)
    up_two, down_two = climb(slope, 2), climb(slope, -2)
    up_three, down_three = climb(up_two, 1), climb(down_two, -1)
    up_four, down_four = climb(up_two[:32], 2), climb(down_two[32:], -2)
    slopes = [up, down, up_two, down_two, up_three, down_three, up_four, down_four]

    turned = call(
        turn_kernel, (shape((2 * BLOCK, ring * 64), BF16),) * 2, [SMEM, VMEM, VMEM], limit=8
    )(place, self_rows, mean)
    keep, send = call(
        gradient_kernel, (shape((n_dom, 8, hidden_width), F32),) * 2, [SMEM] + [VMEM] * 11, limit=16
    )(place, *turned, slope, *slopes)
    partial = call(add_kernel, shape(keep.shape, F32), [VMEM, VMEM], limit=4)(
        keep, lax.ppermute(send, "feat", across)
    )
    shares = lax.all_to_all(partial, "dom", split_axis=0, concat_axis=0, tiled=True)
    total = call(sum_kernel, shape(shares.shape, F32), [VMEM], limit=4)(shares)
    grads = lax.all_to_all(
        total, "dom", split_axis=0, concat_axis=0, tiled=True
    ).reshape(n_dom * 8, hidden_width)
    return hidden, grads[: n_dom * 4], grads[n_dom * 4 :]


def solution(mesh):
    return jax.shard_map(
        body,
        mesh=mesh,
        in_specs=(
            P("feat", "dom"),
            P("dom"),
            P(None, "dom"),
            P("dom", None),
            P("dom"),
            P("dom"),
            P("feat", None),
            P("feat", None),
            P(),
            P(("dom", "feat"), None),
        ),
        out_specs=(P(("dom", "feat"), None), P("feat", None), P("feat", None)),
        check_vma=False,
    )
```

```python
import functools

import jax
import jax.numpy as jnp
from jax import lax
from jax.experimental import pallas as pl
from jax.experimental.pallas import tpu as pltpu
from jax.sharding import PartitionSpec as P

FAN = 15
BLOCK = 128
SLOTS = 8
HALF = BLOCK // 2
DISTANCES = (0, 1, -1, 2, -2, 3, -3, 4)
F32 = jnp.float32
BF16 = jnp.bfloat16
SMEM = pl.BlockSpec(memory_space=pltpu.SMEM)
VMEM = pl.BlockSpec(memory_space=pltpu.VMEM)
ANY = pl.BlockSpec(memory_space=pl.ANY)


def lane_of(shape):
    return lax.broadcasted_iota(jnp.int32, shape, len(shape) - 1)


def split(value):
    high = value.astype(BF16)
    low = (value - high.astype(F32)).astype(BF16)
    return high, low


def dot(left, right):
    return jnp.dot(left, right, preferred_element_type=F32)


def prepare_kernel(
    core_ref, seed_hbm, table_hbm, packed_ref, keep_ref, send_ref,
    rows, table, seed_ref, packed, sems, seed_sem, out_sems,
):
    core = core_ref[0]
    parts = sems.shape[0]
    width = table.shape[1] // parts
    pairs = width // (2 * BLOCK)
    first = lane_of((HALF, BLOCK)) < HALF

    def fetch(part):
        window = pl.ds(part * width, width)
        return pltpu.make_async_copy(table_hbm.at[:, window], table.at[:, window], sems.at[part])

    seeds = pltpu.make_async_copy(seed_hbm, seed_ref, seed_sem)
    seeds.start()
    for part in range(parts):
        fetch(part).start()

    def turn(pair, carry):
        start = pl.multiple_of(pair * 2 * BLOCK, 2 * BLOCK)
        left = table[:, pl.ds(start, BLOCK)]
        right = table[:, pl.ds(start + BLOCK, BLOCK)]
        turned = jnp.concatenate([left, right], axis=0).T
        rows[pl.ds(start, BLOCK), :] = turned
        rows[pl.ds(start + BLOCK, BLOCK), :] = pltpu.roll(turned, HALF, 1)
        for which in range(2):
            near = pl.multiple_of(start + which * BLOCK + core * HALF, HALF)
            far = pl.multiple_of(start + (1 - which) * BLOCK + (1 - core) * HALF, HALF)
            both_halves = jnp.where(first, rows[pl.ds(near, HALF), :], rows[pl.ds(far, HALF), :])
            packed[2 * pair + which] = both_halves.astype(BF16)
        return carry

    outs = []
    for part in range(parts):
        fetch(part).wait()
        lax.fori_loop(part * pairs, (part + 1) * pairs, turn, 0, unroll=pairs)
        window = pl.ds(2 * pairs * part, 2 * pairs)
        outs.append(pltpu.make_async_copy(packed.at[window], packed_ref.at[window], out_sems.at[part]))
        outs[-1].start()
    seeds.wait()

    def pick(chip, carry):
        for mine, ref in ((True, keep_ref), (False, send_ref)):
            base = (2 * chip + (core if mine else 1 - core)) * 64
            for step in range(64):
                ref[chip, pl.ds(step, 1), :] = rows[pl.ds(seed_ref[base + step], 1), :]
        return carry

    lax.fori_loop(0, keep_ref.shape[0], pick, 0)
    for copy in outs:
        copy.wait()


def pack_kernel(
    request_hbm, packed_hbm, self_hbm, neigh_hbm, out_hbm, weight_hbm,
    wanted, packed_ref, both, weight_ref, out_ref, sem, in_sem, out_sems, weight_sems,
):
    slots = pltpu.make_async_copy(request_hbm, wanted, sem)
    slots.start()
    fetch = pltpu.make_async_copy(packed_hbm, packed_ref, in_sem)
    fetch.start()
    weights = [
        pltpu.make_async_copy(ref, both.at[which], weight_sems.at[which])
        for which, ref in enumerate((self_hbm, neigh_hbm))
    ]
    for copy in weights:
        copy.start()
    for held in weights:
        held.wait()
    high, low = split(both[0])
    weight_ref[0] = high
    weight_ref[1] = low
    weight_ref[2] = both[1].astype(BF16)
    copies = [pltpu.make_async_copy(weight_ref, weight_hbm, weight_sems.at[2])]
    copies[0].start()
    slots.wait()
    fetch.wait()
    for part in range(out_ref.shape[0]):
        for slot in range(SLOTS):
            out_ref[part, slot] = packed_ref[wanted[part, 0, slot]]
        copies.append(pltpu.make_async_copy(out_ref.at[part], out_hbm.at[part], out_sems.at[part]))
        copies[-1].start()
    for copy in copies:
        copy.wait()


def collect_kernel(first, owner_ref, arrived_ref, *rest):
    out_ref, seen = rest[-2:]
    for owner in range(arrived_ref.shape[0] // SLOTS):
        seen[owner] = 0

    def skip(entry, carry):
        owner = owner_ref[entry]
        seen[owner] = seen[owner] + 1
        return carry

    def place(entry, carry):
        owner = owner_ref[first + entry]
        rank = seen[owner]
        seen[owner] = rank + 1
        out_ref[entry] = arrived_ref[owner * SLOTS + rank]
        return carry

    if first:
        lax.fori_loop(0, first, skip, 0, unroll=8)
    lax.fori_loop(0, out_ref.shape[0], place, 0, unroll=8)


def gather_kernel(core_ref, count_ref, near_hbm, own_a, own_b, other_a, other_b, out_ref, front, near_ref, sem):
    core = core_ref[0]
    fetch = pltpu.make_async_copy(near_hbm, near_ref, sem)
    fetch.start()
    lane = lane_of((HALF, BLOCK))
    row = lax.broadcasted_iota(jnp.int32, (HALF, BLOCK), 0)
    straight = (lane < HALF) == (core == 0)

    def place(first, own_ref, other_ref, step, carry):
        entry = first + step
        own = own_ref[step].astype(F32)
        other = other_ref[step].astype(F32)
        count = count_ref[entry]
        upper = jnp.where(straight, own, other)
        lower = pltpu.roll(jnp.where(straight, other, own), HALF, 1)
        start = pl.multiple_of(entry * BLOCK, BLOCK)
        front[pl.ds(start, HALF), :] = jnp.where(row < count, upper, 0.0)
        front[pl.ds(start + HALF, HALF), :] = jnp.where(row < count - HALF, lower, 0.0)
        return carry

    half = own_a.shape[0]
    for first, pair in ((0, (own_a, other_a)), (half, (own_b, other_b))):
        lax.fori_loop(0, half, functools.partial(place, first, *pair), 0, unroll=8)
    fetch.wait()

    def average(step, carry):
        group, part = lax.div(step, 2), lax.rem(step, 2)
        base = ((2 * group + core) * 64 + part * 32) * FAN
        for seed in range(32):
            terms = [front[pl.ds(near_ref[base + seed * FAN + k], 1), :] for k in range(FAN)]
            while len(terms) > 1:
                terms = [
                    terms[i] + terms[i + 1] if i + 1 < len(terms) else terms[i]
                    for i in range(0, len(terms), 2)
                ]
            out_ref[group, pl.ds(part * 32 + seed, 1), :] = terms[0] * (1.0 / FAN)
        return carry

    lax.fori_loop(0, 16, average, 0)


def join_kernel(place_ref, own_ref, other_ref, *rest):
    out_ref, sends = rest[0], rest[1:]
    lane = lane_of((64, BLOCK)) < HALF
    first = place_ref[0] == 0
    ring = own_ref.shape[0]
    for shift in range(ring):
        group = lax.rem(place_ref[1] + shift, ring)
        own, other = own_ref[group], other_ref[group]
        left, right = jnp.where(first, own, other), jnp.where(first, other, own)
        joined = jnp.where(lane, left, pltpu.roll(right, HALF, 1))
        out_ref[group] = joined
        sends[shift][...] = joined


def open_kernel(owner_ref, block_ref, request_ref):
    parts = request_ref.shape[0]
    wide = (parts, owner_ref.shape[1])
    owner = jnp.broadcast_to(owner_ref[...], wide)
    block = jnp.broadcast_to(block_ref[...], wide).astype(F32)
    mine = owner == lax.broadcasted_iota(jnp.int32, wide, 0)
    square = (wide[1], wide[1])
    below = lax.broadcasted_iota(jnp.int32, square, 0) <= lane_of(square)
    rank = dot(mine.astype(BF16), below.astype(BF16))
    lane = lane_of((parts, BLOCK))
    result = jnp.zeros((parts, BLOCK), F32)
    for slot in range(SLOTS):
        hit = jnp.logical_and(mine, rank == slot + 1.0)
        chosen = jnp.sum(jnp.where(hit, block, 0.0), axis=1, keepdims=True)
        result = jnp.where(lane == slot, chosen, result)
    result = result.astype(jnp.int32)
    for part in range(parts):
        request_ref[part] = result[part : part + 1]


def three(left, right_high, right_low):
    high, low = split(left)
    return dot(high, right_high) + (dot(high, right_low) + dot(low, right_high))


def self_kernel(place_ref, bias_ref, weight_hbm, *rest):
    pieces = rest[:8]
    part_ref, neigh_ref, held, rows, sems, row_sems = rest[8:]
    chips = [lax.rem(place_ref[1] + 8 - distance, 8) for distance in DISTANCES]
    copies, row_copies = [], []
    for index, (piece, chip) in enumerate(zip(pieces, chips)):
        row_copies.append(pltpu.make_async_copy(piece, rows.at[index], row_sems.at[index]))
        row_copies[-1].start()
        pair = weight_hbm.at[pl.ds(2 * chip, 2), pl.ds(0, 2)]
        copies.append(pltpu.make_async_copy(pair, held.at[index], sems.at[index]))
        copies[-1].start()
    neigh_copies = []
    for step in range(4):
        window = pl.ds(4 * step, 4)
        neigh_copies.append(
            pltpu.make_async_copy(weight_hbm.at[window, 2], neigh_ref.at[window], sems.at[8 + step])
        )
        neigh_copies[-1].start()
    total = jnp.broadcast_to(bias_ref[...], part_ref.shape)
    for step in range(4):
        pair = (2 * step, 2 * step + 1)
        for index in pair:
            copies[index].wait()
            row_copies[index].wait()
        left = jnp.concatenate([rows[index] for index in pair], axis=1)
        high, low = [
            jnp.concatenate([held[index, core, which] for index in pair for core in range(2)], axis=0)
            for which in range(2)
        ]
        total = total + three(left, high, low)
    part_ref[...] = total
    for copy in neigh_copies:
        copy.wait()


def forward_kernel(mean_ref, part_ref, weight_ref, cotangent_ref, hidden_ref, slope_ref):
    preact = part_ref[...]
    for step in range(4):
        left = jnp.concatenate([mean_ref[2 * step], mean_ref[2 * step + 1]], axis=1)
        right = weight_ref[4 * step : 4 * step + 4].reshape(256, weight_ref.shape[2])
        for piece in split(left):
            preact = preact + dot(piece, right)
    sigma = 1.0 / (1.0 + jnp.exp(-preact))
    hidden_ref[...] = (preact * sigma).astype(BF16)
    slope = cotangent_ref[...].astype(F32) * (sigma * (1.0 + preact * (1.0 - sigma)))
    slope_ref[...] = slope.astype(BF16)


def turn_kernel(place_ref, self_ref, mean_ref, high_ref, low_ref):
    rows = [lax.rem(place_ref[1] + 8 - k, 8) for k in DISTANCES]
    for which, ref in enumerate((self_ref, mean_ref)):
        turned = jnp.concatenate([ref[r] for r in rows], axis=0).T
        window = slice(which * BLOCK, (which + 1) * BLOCK)
        high_ref[window], low_ref[window] = split(turned)


def gradient_kernel(place_ref, high_ref, low_ref, near_ref, *rest):
    slopes, (keep_ref, send_ref) = rest[:-2], rest[-2:]
    right = jnp.concatenate([near_ref[...]] + [ref[...] for ref in slopes], axis=0)
    first = place_ref[0] == 0
    for which in range(2):
        window = slice(which * BLOCK, (which + 1) * BLOCK)
        total = dot(high_ref[window], right) + dot(low_ref[window], right)
        for chunk in range(8):
            start = chunk * 8
            one, two = total[start : start + 8], total[64 + start : 64 + start + 8]
            keep_ref[which * 8 + chunk] = jnp.where(first, one, two)
            send_ref[which * 8 + chunk] = jnp.where(first, two, one)


def add_kernel(left_ref, right_ref, out_ref):
    out_ref[...] = left_ref[...] + right_ref[...]


def sum_kernel(in_ref, out_ref):
    total = in_ref[0]
    for i in range(1, in_ref.shape[0]):
        total = total + in_ref[i]
    for i in range(out_ref.shape[0]):
        out_ref[i] = total


def call(kernel, shapes, specs, scratch=(), limit=8, cost=None, outs=None, aliases={}):
    return pl.pallas_call(
        kernel,
        out_shape=shapes,
        in_specs=specs,
        out_specs=outs or jax.tree.map(lambda _: VMEM, shapes),
        input_output_aliases=aliases,
        scratch_shapes=list(scratch),
        cost_estimate=cost,
        compiler_params=pltpu.CompilerParams(vmem_limit_bytes=int(limit * (1 << 20))),
    )


def cost(flops, size):
    return pl.CostEstimate(flops=flops, bytes_accessed=size, transcendentals=0)


def body(
    feature_table,
    seed_ids,
    neighbours,
    owners,
    blocks,
    counts,
    w_self,
    w_neigh,
    out_bias,
    cotangent,
):
    n_dom = lax.axis_size("dom")
    n_feat = lax.axis_size("feat")
    ring = n_feat // 2
    across = [(i, i ^ 1) for i in range(n_feat)]
    columns = [[2 * z + c for z in range(ring)] for c in range(2)]
    feat = lax.axis_index("feat").astype(jnp.int32).reshape(1)
    core = feat % 2
    place = jnp.concatenate([core, feat // 2])
    hidden_width = w_self.shape[1]

    def climb(value, chips):
        pairs = [(i, (i + 2 * chips) % n_feat) for i in range(n_feat)]
        return lax.ppermute(value, "feat", pairs)

    owner_ids = owners[:, 0]
    shape = jax.ShapeDtypeStruct

    request = call(
        open_kernel, shape((n_dom, 1, BLOCK), jnp.int32), [VMEM, VMEM], limit=60
    )(owner_ids[None, :], blocks[None, :])
    requests = lax.all_to_all(request, "dom", split_axis=0, concat_axis=0, tiled=True)
    near = jnp.transpose(neighbours).reshape(-1)
    packed, kept, given = call(
        prepare_kernel,
        (
            shape((feature_table.shape[1] // BLOCK, HALF, BLOCK), BF16),
            shape((ring, 64, BLOCK), F32),
            shape((ring, 64, BLOCK), F32),
        ),
        [SMEM, ANY, ANY],
        [
            pltpu.VMEM((feature_table.shape[1], BLOCK), F32),
            pltpu.VMEM(feature_table.shape, F32),
            pltpu.SMEM(seed_ids.shape, jnp.int32),
            pltpu.VMEM((feature_table.shape[1] // BLOCK, HALF, BLOCK), BF16),
            pltpu.SemaphoreType.DMA((8,)),
            pltpu.SemaphoreType.DMA,
            pltpu.SemaphoreType.DMA((8,)),
        ],
        limit=60, cost=cost(0, 10 << 20), outs=(ANY, VMEM, VMEM),
    )(core, seed_ids, feature_table)

    outgoing, weight = call(
        pack_kernel,
        (shape((n_dom, SLOTS, HALF, BLOCK), BF16), shape((3, 64, hidden_width), BF16)),
        [ANY] * 4,
        [
            pltpu.SMEM((n_dom, 1, BLOCK), jnp.int32),
            pltpu.VMEM(packed.shape, BF16),
            pltpu.VMEM((2, 64, hidden_width), F32),
            pltpu.VMEM((3, 64, hidden_width), BF16),
            pltpu.VMEM((n_dom, SLOTS, HALF, BLOCK), BF16),
            pltpu.SemaphoreType.DMA,
            pltpu.SemaphoreType.DMA,
            pltpu.SemaphoreType.DMA((n_dom,)),
            pltpu.SemaphoreType.DMA((3,)),
        ],
        limit=53.8, outs=(ANY, ANY),
    )(requests, packed, w_self, w_neigh)
    weights = lax.all_gather(weight, "feat", axis=0, tiled=False)
    arrived = lax.all_to_all(
        outgoing.reshape(n_dom, SLOTS * HALF, BLOCK), "dom", split_axis=0, concat_axis=0, tiled=True
    )
    self_rows, *sends = call(
        join_kernel,
        (shape((ring, 64, BLOCK), F32),) + (shape((64, BLOCK), F32),) * ring,
        [SMEM, VMEM, VMEM],
        limit=53.55, cost=cost(0, 1 << 20),
    )(place, kept, lax.ppermute(given, "feat", across))
    moved = [climb(sends[k % ring], k) for k in DISTANCES[1:]]
    pieces = [sends[0]] + moved

    half = owner_ids.shape[0] // 2
    blocks_here = arrived.reshape(n_dom * SLOTS, HALF, BLOCK)
    entries = [
        call(
            functools.partial(collect_kernel, first), shape((half, HALF, BLOCK), BF16),
            [SMEM, VMEM] + [ANY] * 8, [pltpu.SMEM((n_dom,), jnp.int32)], limit=2, cost=cost(0, 1 << 20),
        )(owner_ids, blocks_here, *moved, near)
        for first in (0, half)
    ]
    swapped = [lax.ppermute(value, "feat", across) for value in entries]
    mean = call(
        gather_kernel,
        shape((ring, 64, BLOCK), F32),
        [SMEM, SMEM, ANY] + [VMEM] * 4,
        [
            pltpu.VMEM((owner_ids.shape[0] * BLOCK, BLOCK), F32),
            pltpu.SMEM(near.shape, jnp.int32),
            pltpu.SemaphoreType.DMA,
        ],
        cost=cost(0, 30 << 20),
    )(core, counts, near, *entries, *swapped)

    part, neigh_weight = call(
        self_kernel,
        (shape((64, hidden_width), F32), shape((n_feat, 64, hidden_width), BF16)),
        [SMEM, VMEM] + [ANY] * 9,
        [
            pltpu.VMEM((ring, 2, 2, 64, hidden_width), BF16),
            pltpu.VMEM((ring, 64, BLOCK), F32),
            pltpu.SemaphoreType.DMA((12,)),
            pltpu.SemaphoreType.DMA((ring,)),
        ],
        limit=51.4, cost=cost(3 << 27, 9 << 20),
    )(place, out_bias[None, :], weights, *pieces)
    mean_seeds = lax.all_to_all(
        mean, "feat", split_axis=0, concat_axis=0, tiled=True, axis_index_groups=columns
    )

    hidden, slope = call(
        forward_kernel,
        (shape((64, hidden_width), BF16), shape((64, hidden_width), BF16)),
        [VMEM] * 4, limit=8, cost=cost(2 << 27, 4 << 20),
    )(mean_seeds, part, neigh_weight, cotangent)

    up, down = climb(slope, 1), climb(slope, -1)
    up_two, down_two = climb(slope, 2), climb(slope, -2)
    up_three, down_three = climb(up_two, 1), climb(down_two, -1)
    up_four, down_four = climb(up_two[:32], 2), climb(down_two[32:], -2)
    slopes = [up, down, up_two, down_two, up_three, down_three, up_four, down_four]

    turned = call(
        turn_kernel, (shape((2 * BLOCK, ring * 64), BF16),) * 2, [SMEM, VMEM, VMEM], limit=8
    )(place, self_rows, mean)
    keep, send = call(
        gradient_kernel, (shape((n_dom, 8, hidden_width), F32),) * 2, [SMEM] + [VMEM] * 11, limit=16
    )(place, *turned, slope, *slopes)
    partial = call(add_kernel, shape(keep.shape, F32), [VMEM, VMEM], limit=4)(
        keep, lax.ppermute(send, "feat", across)
    )
    shares = lax.all_to_all(partial, "dom", split_axis=0, concat_axis=0, tiled=True)
    total = call(sum_kernel, shape(shares.shape, F32), [VMEM], limit=4)(shares)
    grads = lax.all_to_all(
        total, "dom", split_axis=0, concat_axis=0, tiled=True
    ).reshape(n_dom * 8, hidden_width)
    return hidden, grads[: n_dom * 4], grads[n_dom * 4 :]


def solution(mesh):
    return jax.shard_map(
        body,
        mesh=mesh,
        in_specs=(
            P("feat", "dom"),
            P("dom"),
            P(None, "dom"),
            P("dom", None),
            P("dom"),
            P("dom"),
            P("feat", None),
            P("feat", None),
            P(),
            P(("dom", "feat"), None),
        ),
        out_specs=(P(("dom", "feat"), None), P("feat", None), P("feat", None)),
        check_vma=False,
    )
```
